32 devices in a mesh: grp: 4 (over x, core), blk: 8 (over z, y).
Axes of the slice: x: 2, y: 2, z: 4, core: 2. Of those that a mesh axis runs over, the one named last changes fastest.
Arguments:
- features: bfloat16 [4, 8, 4096, 256], P('grp', 'blk'), may hold values from -6 to 6
- hub_rows: int32 [4, 8, 32], P('grp', 'blk'), may hold values from 0 to 4095
- hub_adjacency: bfloat16 [4, 8, 4096, 256], P('grp', 'blk'), as said below
- tile_row: int32 [4, 8, 160], P('grp', 'blk'), may hold values from 0 to 31
- tile_col: int32 [4, 8, 160], P('grp', 'blk'), may hold values from 0 to 39
- tile_count: int32 [4, 8], P('grp', 'blk'), may hold values from 26 to 160, as said below
- tile_values: bfloat16 [4, 8, 160, 128, 128], P('grp', 'blk'), may hold values from 0 to 0.049804688
- send_rows: int32 [4, 8, 4, 8, 32], P('grp', 'blk'), may hold values from 0 to 4095
- weight: bfloat16 [256, 256], replicated, may hold values from -0.375 to 0.375
Outputs:
- activations: bfloat16 [4, 8, 4096, 256], P('grp', 'blk')
The draws below stay inside these ranges and needn't reach their ends.
Inputs may be any that keep to these rules, and one draw needn't show every extreme that they name: `tile_count`: some device has exactly 160 live tile slots in every draw. `hub_adjacency`: Non-negative edge weights.
All inputs are finite; a program needn't handle non-finite values.
Results may differ from the reference program's by a relative error of at most 0.0014.
The reference program's roundings to bfloat16 on the way (of `hub_feats`, `received` and `aggregated`) count: a program that leaves them out, or rounds other values in their place, can miss the bound.
Values may be sent and summed in bfloat16 or wider, within the bound.
A program may use at most 128 MiB of HBM per device.

```python
import jax
import jax.numpy as jnp
from jax import lax

FEAT = 256
ROWS_DEV = 4096
TB = 128
HUB_DEV = 32
SEND = 32
MAXT = 160
HUBS = 256
RECV = 1024
N_GRP = 4
N_BLK = 8


def draw_hub_adjacency(key, part):
    base = jax.random.uniform(key, (N_GRP, N_BLK, ROWS_DEV, HUBS), jnp.float32)
    factor = (3.0 / HUBS) ** 0.5
    return (base * factor).astype(jnp.bfloat16)


def draw_tile_count(key, part):
    total = N_GRP * N_BLK
    divisor = jax.random.randint(key, (total,), 1, 7)
    counts = MAXT // divisor
    busiest = jax.random.randint(jax.random.fold_in(key, 3), (), 0, total)
    counts = jnp.where(jnp.arange(total) == busiest, MAXT, counts)
    return counts.reshape(N_GRP, N_BLK).astype(jnp.int32)


def place_ends(values, key, smallest, largest):
    longest = values.shape.index(max(values.shape))
    spots = []
    for shift in (0, 1):
        where = [jax.random.randint(jax.random.fold_in(key, axis), (), 0, length) for axis, length in enumerate(values.shape)]
        where[longest] = (where[longest] + shift) % values.shape[longest]
        spots.append(tuple(where))
    return values.at[spots[0]].set(smallest).at[spots[1]].set(largest)


def steps_of(own_key, extent, cuts, least, largest):
    def one(axis_at, parts):
        heights = jax.random.uniform(jax.random.fold_in(jax.random.fold_in(own_key, 6), axis_at), (parts,), jnp.float32, least / len(cuts), largest / len(cuts))
        return jnp.repeat(jnp.exp(heights), extent[axis_at] // parts).reshape((-1,) + (1,) * (len(extent) - axis_at - 1))

    gain = one(*cuts[0])
    for cut in cuts[1:]:
        gain = gain * one(*cut)
    return gain


def scatter_about(key, dims, scale, most, shards=(), kind=jnp.bfloat16):
    values = scale * jax.random.normal(key, dims, jnp.float32)
    if shards:
        values = values * steps_of(key, dims, shards, -0.22, 0.18)
    return jnp.clip(values, -most, most).astype(kind)


def setup_inputs(seed: int = 0) -> dict:
    arg_keys = jax.random.split(jax.random.key(seed), 10)
    return {
        "features": scatter_about(arg_keys[0], (N_GRP, N_BLK, ROWS_DEV, FEAT), 1.0, 6.0, ((0, 4), (1, 8))),
        "hub_rows": place_ends(jax.random.randint(arg_keys[1], (N_GRP, N_BLK, HUB_DEV), 0, ROWS_DEV), jax.random.fold_in(arg_keys[1], 1), 0, ROWS_DEV - 1).astype(jnp.int32),
        "hub_adjacency": draw_hub_adjacency(jax.random.fold_in(arg_keys[9], 71), 0),
        "tile_row": place_ends(jax.random.randint(arg_keys[3], (N_GRP, N_BLK, MAXT), 0, ROWS_DEV // TB), jax.random.fold_in(arg_keys[3], 1), 0, (ROWS_DEV // TB) - 1).astype(jnp.int32),
        "tile_col": place_ends(jax.random.randint(arg_keys[4], (N_GRP, N_BLK, MAXT), 0, (ROWS_DEV + RECV) // TB), jax.random.fold_in(arg_keys[4], 1), 0, ((ROWS_DEV + RECV) // TB) - 1).astype(jnp.int32),
        "tile_count": draw_tile_count(jax.random.fold_in(arg_keys[9], 71), 0),
        "tile_values": jnp.clip(0.049804688 * jax.random.uniform(arg_keys[6], (N_GRP, N_BLK, MAXT, TB, TB), jnp.float32) ** steps_of(arg_keys[6], (N_GRP, N_BLK, MAXT, TB, TB), ((0, 4), (1, 8)), -0.2, 0.2), 0.0, 0.049804688).astype(jnp.bfloat16),
        "send_rows": place_ends(jax.random.randint(arg_keys[7], (N_GRP, N_BLK, N_GRP, N_BLK, SEND), 0, ROWS_DEV), jax.random.fold_in(arg_keys[7], 1), 0, ROWS_DEV - 1).astype(jnp.int32),
        "weight": scatter_about(arg_keys[8], (FEAT, FEAT), FEAT ** -0.5, 0.375),
    }


def pick_rows(table, index):
    return table[index]


def reference(features, hub_rows, hub_adjacency, tile_row, tile_col, tile_count, tile_values, send_rows, weight):
    devices = N_GRP * N_BLK
    hub_feats = jax.vmap(jax.vmap(pick_rows))(features, hub_rows.astype(jnp.int32))
    hub_group = hub_feats.reshape(N_GRP, HUBS, FEAT)
    sent = jax.vmap(jax.vmap(pick_rows))(features, send_rows.astype(jnp.int32))
    received = jnp.transpose(sent, (2, 3, 0, 1, 4, 5)).reshape(devices, RECV, FEAT)
    group = (jnp.arange(devices, dtype=jnp.int32) // N_BLK).astype(jnp.int32)

    def one_device(item):
        local, adjacency, incoming, rows, cols, count, values, owner = item
        hub_part = jnp.dot(adjacency, hub_group[owner], preferred_element_type=jnp.float32)
        table = jnp.concatenate([local, incoming], 0).reshape(-1, TB, FEAT)
        picked = table[cols]
        products = jnp.einsum("tij,tjf->tif", values.astype(jnp.float32), picked.astype(jnp.float32))
        valid = (jnp.arange(MAXT, dtype=jnp.int32) < count).astype(jnp.float32)
        summed = jax.ops.segment_sum(products * valid[:, None, None], rows, num_segments=ROWS_DEV // TB)
        aggregated = (hub_part + summed.reshape(ROWS_DEV, FEAT)).astype(jnp.bfloat16)
        mixed = jnp.dot(aggregated, weight, preferred_element_type=jnp.float32)
        return jnp.maximum(mixed, 0.0).astype(jnp.bfloat16)

    items = (features.reshape(devices, ROWS_DEV, FEAT),
             hub_adjacency.reshape(devices, ROWS_DEV, HUBS),
             received,
             tile_row.reshape(devices, MAXT).astype(jnp.int32),
             tile_col.reshape(devices, MAXT).astype(jnp.int32),
             tile_count.reshape(devices).astype(jnp.int32),
             tile_values.reshape(devices, MAXT, TB, TB),
             group)
    result = lax.map(one_device, items)
    return result.reshape(N_GRP, N_BLK, ROWS_DEV, FEAT)
```

```python
import functools

import jax
import jax.numpy as jnp
from jax import lax
from jax.experimental import pallas as pl
from jax.experimental.pallas import tpu as pltpu
from jax.sharding import PartitionSpec as P

TB = 128
MESH = pl.DeviceIdType.MESH
ANY = pl.BlockSpec(memory_space=pl.ANY)
VMEM = pl.BlockSpec(memory_space=pltpu.VMEM)
SMEM = pl.BlockSpec(memory_space=pltpu.SMEM)


def pick(listing, feats_ref):
    lists, entries = listing.shape
    rows, width = feats_ref.shape
    count = lists * entries
    step = 512
    wide = jnp.broadcast_to(listing[:, :, None], (lists, entries, step)).reshape(count, step)
    lane = lax.broadcasted_iota(jnp.int32, (count, step), 1)
    offset = wide - lane
    total = jnp.zeros((count, width), jnp.float32)
    for at in range(0, rows, step):
        chosen = jnp.where(offset == at, 1.0, 0.0).astype(jnp.bfloat16)
        total += jnp.dot(chosen, feats_ref[at : at + step, :], preferred_element_type=jnp.float32)
    return total.astype(jnp.bfloat16)


def exchange_kernel(
    groups, blocks, feats_ref, hub_rows_ref, send_rows_ref,
    received_ref, hub_ref,
    stage, hub_stage, send_sem, recv_sem, hub_send_sem, hub_recv_sem, own_sem,
):
    g = lax.axis_index("grp")
    b = lax.axis_index("blk")
    entries = send_rows_ref.shape[2]
    hubs = hub_stage.shape[0]
    half = blocks // 2
    me = g * blocks + b

    barrier = pltpu.get_barrier_semaphore()
    devices = groups * blocks

    def greet(off, _):
        other = lax.rem(me + off, devices)
        pl.semaphore_signal(
            barrier, inc=1, device_id=(other // blocks, lax.rem(other, blocks)), device_id_type=MESH
        )
        return 0

    lax.fori_loop(1, devices, greet, 0)

    def boundary_copy(j, k, dst_g, dst_b, slot):
        return pltpu.make_async_remote_copy(
            src_ref=stage.at[dst_g * blocks + dst_b],
            dst_ref=received_ref.at[slot],
            send_sem=send_sem.at[j, k],
            recv_sem=recv_sem.at[j, k],
            device_id=(dst_g, dst_b),
            device_id_type=MESH,
        )

    def hub_copy(k, dst_b, src_b):
        return pltpu.make_async_remote_copy(
            src_ref=hub_stage,
            dst_ref=hub_ref.at[src_b],
            send_sem=hub_send_sem.at[k],
            recv_sem=hub_recv_sem.at[k],
            device_id=(g, dst_b),
            device_id_type=MESH,
        )

    def gather(j):
        dst_g = lax.rem(g + j, groups)
        rows = pick(send_rows_ref[dst_g], feats_ref)
        stage[pl.ds(dst_g * blocks, blocks)] = rows.reshape(blocks, entries, rows.shape[1])
        return dst_g

    def send(j, dst_g):
        def one(k, _):
            dst_b = lax.rem(b + half + k, blocks)

            @pl.when((dst_g != g) | (dst_b != b))
            def _():
                boundary_copy(j, k, dst_g, dst_b, me).start()

            return 0

        lax.fori_loop(0, blocks, one, 0)

    hub_stage[...] = pick(hub_rows_ref[...], feats_ref)
    pl.semaphore_wait(barrier, devices - 1)
    for k in range(1, blocks):
        hub_copy(k, lax.rem(b + k, blocks), b).start()
    own_hub = pltpu.make_async_copy(hub_stage, hub_ref.at[b], own_sem.at[0])
    own_hub.start()

    def chunk(j, _):
        send(j, gather(j))
        return 0

    lax.fori_loop(0, groups, chunk, 0)
    own = pltpu.make_async_copy(stage.at[me], received_ref.at[me], own_sem.at[1])
    own.start()

    for k in range(1, blocks):
        src_b = lax.rem(b + blocks - k, blocks)
        arrived = hub_copy(k, lax.rem(b + k, blocks), src_b)
        arrived.wait_send()
        arrived.wait_recv()
    own_hub.wait()

    def finish(at, _):
        j = at // blocks
        k = lax.rem(at, blocks)
        src_g = lax.rem(g + groups - j, groups)
        src_b = lax.rem(b + 2 * blocks - half - k, blocks)

        @pl.when((src_g != g) | (src_b != b))
        def _():
            arrived = boundary_copy(
                j, k, lax.rem(g + j, groups), lax.rem(b + half + k, blocks), src_g * blocks + src_b
            )
            arrived.wait_send()
            arrived.wait_recv()

        return 0

    lax.fori_loop(0, devices, finish, 0)
    own.wait()


def local_kernel(
    count_ref, row_ref, col_ref, feats_hbm, received_hbm, hub_hbm, adj_hbm, tiles_hbm, weight_hbm,
    out_hbm,
    table, hub, adj, tiles, weight, total, result, in_sem, tile_sem, out_sem,
):
    rows = feats_hbm.shape[0]
    slots = tiles_hbm.shape[0]
    row_blocks = rows // TB
    part = 16
    parts = slots // part
    live = count_ref[0]

    copies = [
        pltpu.make_async_copy(hub_hbm, hub, in_sem.at[0]),
        pltpu.make_async_copy(adj_hbm, adj, in_sem.at[1]),
        pltpu.make_async_copy(feats_hbm, table.at[pl.ds(0, rows)], in_sem.at[2]),
        pltpu.make_async_copy(received_hbm, table.at[pl.ds(rows, received_hbm.shape[0])], in_sem.at[3]),
        pltpu.make_async_copy(weight_hbm, weight, in_sem.at[4]),
    ]

    def tile_copy(c):
        at = pl.ds(c * part, part)
        return pltpu.make_async_copy(tiles_hbm.at[at], tiles.at[at], tile_sem.at[c])

    for copy in copies:
        copy.start()
    for c in range(parts):
        tile_copy(c).start()

    copies[0].wait()
    copies[1].wait()

    @pl.loop(0, rows // 256)
    def _(i):
        at = pl.ds(i * 256, 256)
        total[at, :] = jnp.dot(adj[at, :], hub[...], preferred_element_type=jnp.float32)

    copies[2].wait()
    copies[3].wait()
    copies[4].wait()

    unroll = 4

    @pl.loop(0, parts)
    def _(c):
        tile_copy(c).wait()
        here = jnp.clip(live - c * part, 0, part)

        @pl.loop(0, (here + unroll - 1) // unroll)
        def _(u):
            products = []
            places = []
            for i in range(unroll):
                t = c * part + u * unroll + i
                from_table = table[pl.ds(pl.multiple_of(col_ref[t] * TB, TB), TB), :]
                products.append(
                    jnp.dot(tiles[t], from_table, preferred_element_type=jnp.float32)
                )
                places.append(jnp.where(t < live, row_ref[t], row_blocks))
            for product, place in zip(products, places):
                at = pl.ds(pl.multiple_of(place * TB, TB), TB)
                total[at, :] += product

    def out_copy(i):
        at = pl.ds(i * 512, 512)
        return pltpu.make_async_copy(result.at[at], out_hbm.at[at], out_sem.at[i])

    for i in range(rows // 512):
        at = slice(i * 512, (i + 1) * 512)
        mixed = jnp.dot(
            total[at, :].astype(jnp.bfloat16), weight[...], preferred_element_type=jnp.float32
        )
        result[at, :] = jnp.maximum(mixed, 0.0).astype(jnp.bfloat16)
        out_copy(i).start()
    for i in range(rows // 512):
        out_copy(i).wait()


def per_device(
    groups, blocks, features, hub_rows, hub_adjacency, tile_row, tile_col, tile_count,
    tile_values, send_rows, weight,
):
    local = features[0, 0]
    rows, width = local.shape
    entries = send_rows.shape[-1]
    hub_dev = hub_rows.shape[-1]
    devices = groups * blocks
    bf16 = jnp.bfloat16
    dma = pltpu.SemaphoreType.DMA
    received, hub = pl.pallas_call(
        functools.partial(exchange_kernel, groups, blocks),
        out_shape=(
            jax.ShapeDtypeStruct((devices, entries, width), bf16),
            jax.ShapeDtypeStruct((blocks, hub_dev, width), bf16),
        ),
        in_specs=[VMEM, VMEM, VMEM],
        out_specs=(ANY, ANY),
        scratch_shapes=[
            pltpu.VMEM((devices, entries, width), bf16),
            pltpu.VMEM((hub_dev, width), bf16),
            dma((groups, blocks)),
            dma((groups, blocks)),
            dma((blocks,)),
            dma((blocks,)),
            dma((2,)),
        ],
        compiler_params=pltpu.CompilerParams(
            collective_id=0, has_side_effects=True, vmem_limit_bytes=48 << 20
        ),
        name="exchange",
    )(local, hub_rows[0], send_rows[0, 0])

    received = received.reshape(devices * entries, width)
    hub = hub.reshape(blocks * hub_dev, width)
    slots = tile_row.shape[-1]
    out = pl.pallas_call(
        local_kernel,
        out_shape=jax.ShapeDtypeStruct((rows, width), bf16),
        in_specs=[SMEM, SMEM, SMEM, ANY, ANY, ANY, ANY, ANY, ANY],
        out_specs=ANY,
        scratch_shapes=[
            pltpu.VMEM((rows + devices * entries, width), bf16),
            pltpu.VMEM((blocks * hub_dev, width), bf16),
            pltpu.VMEM((rows, blocks * hub_dev), bf16),
            pltpu.VMEM((slots, TB, TB), bf16),
            pltpu.VMEM(weight.shape, bf16),
            pltpu.VMEM((rows + TB, width), jnp.float32),
            pltpu.VMEM((rows, width), bf16),
            dma((5,)),
            dma((slots // 16,)),
            dma((rows // 512,)),
        ],
        compiler_params=pltpu.CompilerParams(vmem_limit_bytes=48 << 20),
        name="layer",
    )(
        tile_count[0], tile_row[0, 0], tile_col[0, 0], local, received, hub,
        hub_adjacency[0, 0], tile_values[0, 0], weight,
    )
    return out[None, None]


def solution(mesh):
    return jax.shard_map(
        functools.partial(per_device, mesh.shape["grp"], mesh.shape["blk"]),
        mesh=mesh,
        in_specs=(
            P("grp", "blk", None, None),
            P("grp", "blk", None),
            P("grp", "blk", None, None),
            P("grp", "blk", None),
            P("grp", "blk", None),
            P("grp", "blk"),
            P("grp", "blk", None, None, None),
            P("grp", "blk", None, None, None),
            P(),
        ),
        out_specs=P("grp", "blk", None, None),
        check_vma=False,
    )
```

```python
import functools

import jax
import jax.numpy as jnp
from jax import lax
from jax.experimental import pallas as pl
from jax.experimental.pallas import tpu as pltpu
from jax.sharding import PartitionSpec as P

TB = 128
MESH = pl.DeviceIdType.MESH
ANY = pl.BlockSpec(memory_space=pl.ANY)
VMEM = pl.BlockSpec(memory_space=pltpu.VMEM)
SMEM = pl.BlockSpec(memory_space=pltpu.SMEM)

PART = 16
GROUP = 4
CHUNK = 512


def pick(listing, feats):
    lists, entries = listing.shape
    blocks, _, width = feats.shape
    count = lists * entries
    wide = jnp.broadcast_to(listing[:, :, None], (lists, entries, CHUNK)).reshape(count, CHUNK)
    offset = wide - lax.broadcasted_iota(jnp.int32, (count, CHUNK), 1)
    total = jnp.zeros((count, width), jnp.float32)
    step = CHUNK // TB
    for at in range(0, blocks, step):
        chosen = jnp.where(offset == at * TB, 1.0, 0.0).astype(jnp.bfloat16)
        part = feats[at : at + step].reshape(CHUNK, width)
        total += jnp.dot(chosen, part, preferred_element_type=jnp.float32)
    return total.astype(jnp.bfloat16)


def exchange_kernel(
    groups, blocks, count_ref, feats_hbm, hub_rows_hbm, send_rows_hbm, adj_hbm, row_hbm, col_hbm, tiles_hbm,
    received_ref, partial_hbm,
    feats, hub_rows, send_rows, adj, row_list, col_list, col_at, tiles, links, last, link_at, last_at,
    stage, hub, steps, partial,
    in_sem, tile_sem, link_sem, out_sem, own_sem,
    send_sem, recv_sem, far_send, far_recv, near_send, near_recv,
):
    g = lax.axis_index("grp")
    b = lax.axis_index("blk")
    entries = send_rows.shape[2]
    hub_dev = hub.shape[1]
    row_blocks, _, width = feats.shape
    slots = tiles.shape[0]
    half = blocks // 2
    me = g * blocks + b
    devices = groups * blocks
    high = b // 2
    low = lax.rem(b, 2)

    barrier = pltpu.get_barrier_semaphore()

    def greet(off, _):
        other = lax.rem(me + off, devices)
        pl.semaphore_signal(
            barrier, inc=1, device_id=(other // blocks, lax.rem(other, blocks)), device_id_type=MESH
        )
        return 0

    ins = [
        pltpu.make_async_copy(hub_rows_hbm, hub_rows, in_sem.at[0]),
        pltpu.make_async_copy(send_rows_hbm, send_rows, in_sem.at[1]),
        pltpu.make_async_copy(feats_hbm, feats, in_sem.at[2]),
        pltpu.make_async_copy(row_hbm, row_list, in_sem.at[3]),
        pltpu.make_async_copy(col_hbm, col_list, in_sem.at[4]),
        pltpu.make_async_copy(col_hbm, col_at, in_sem.at[5]),
        pltpu.make_async_copy(adj_hbm, adj, in_sem.at[6]),
    ]

    def tile_copy(c):
        at = pl.ds(c * PART, PART)
        return pltpu.make_async_copy(tiles_hbm.at[at], tiles.at[at], tile_sem.at[c])

    for copy in ins[:6]:
        copy.start()
    lax.fori_loop(1, devices, greet, 0)
    for copy in ins[:3]:
        copy.wait()

    def boundary_copy(j, k, dst_g, dst_b, slot):
        return pltpu.make_async_remote_copy(
            src_ref=stage.at[dst_g * blocks + dst_b],
            dst_ref=received_ref.at[slot],
            send_sem=send_sem.at[j, k],
            recv_sem=recv_sem.at[j, k],
            device_id=(dst_g, dst_b),
            device_id_type=MESH,
        )

    def far_high(k):
        return lax.rem(high + half - k, half)

    def far_copy(k, block):
        return pltpu.make_async_remote_copy(
            src_ref=hub.at[block],
            dst_ref=hub.at[block],
            send_sem=far_send.at[k],
            recv_sem=far_recv.at[k],
            device_id=(g, lax.rem(high + k, half) * 2 + low),
            device_id_type=MESH,
        )

    def near_copy(k, block):
        return pltpu.make_async_remote_copy(
            src_ref=hub.at[block],
            dst_ref=hub.at[block],
            send_sem=near_send.at[k],
            recv_sem=near_recv.at[k],
            device_id=(g, high * 2 + 1 - low),
            device_id_type=MESH,
        )

    def place(dst_g, rows):
        stage[pl.ds(dst_g * blocks, blocks)] = rows.reshape(blocks, entries, width)

    def send(j, dst_g):
        def one(k, _):
            dst_b = lax.rem(b + half + k, blocks)

            @pl.when((dst_g != g) | (dst_b != b))
            def _():
                boundary_copy(j, k, dst_g, dst_b, me).start()

            return 0

        lax.fori_loop(0, blocks, one, 0)

    def chunk(j, _):
        dst_g = lax.rem(g + j, groups)
        place(dst_g, pick(send_rows[dst_g], feats))
        send(j, dst_g)
        return 0

    first_g = lax.rem(g + 1, groups)
    rows = pick(jnp.concatenate([send_rows[first_g], hub_rows[...]], 0), feats)
    place(first_g, rows[: blocks * entries])
    hub[b] = rows[blocks * entries :]
    pl.semaphore_wait(barrier, devices - 1)
    for k in range(1, half):
        far_copy(k, b).start()
    near_copy(0, b).start()
    send(1, first_g)
    ins[6].start()
    for c in range(slots // PART):
        tile_copy(c).start()
    lax.fori_loop(2, groups, chunk, 0)
    chunk(0, 0)
    own = pltpu.make_async_copy(stage.at[me], received_ref.at[me], own_sem)
    own.start()

    for copy in ins[3:6]:
        copy.wait()
    live = (lax.broadcasted_iota(jnp.int32, (1, slots), 1) < count_ref[0]) & (col_list[...] < row_blocks)
    key = jnp.where(live, row_list[...], -1)
    key = jnp.broadcast_to(key[:, :, None], (1, slots, slots)).reshape(slots, slots)
    slot = lax.broadcasted_iota(jnp.int32, (slots, slots), 0)
    place_at = lax.broadcasted_iota(jnp.int32, (slots, slots), 1)

    def latest(hit):
        found = jnp.max(jnp.where(hit, slot, -1), axis=0, keepdims=True)
        return jnp.where(found < 0, slots, found)

    links[...] = latest((key == row_list[...]) & (slot < place_at))
    last[...] = latest(key == place_at)
    to_smem = [
        pltpu.make_async_copy(links, link_at, link_sem.at[0]),
        pltpu.make_async_copy(last, last_at, link_sem.at[1]),
    ]
    for copy in to_smem:
        copy.start()

    for k in range(1, half):
        block = far_high(k) * 2 + low
        far_copy(k, block).wait_recv()
        near_copy(k, block).start()

    steps[slots] = jnp.zeros((TB, width), jnp.float32)
    for copy in to_smem:
        copy.wait()

    def part(c, _):
        tile_copy(c).wait()

        def group(u, _):
            products = []
            for i in range(GROUP):
                t = c * PART + u * GROUP + i
                block = feats[jnp.clip(col_at[0, t], 0, row_blocks - 1)]
                products.append(jnp.dot(tiles[t], block, preferred_element_type=jnp.float32))
            for i in range(GROUP):
                t = c * PART + u * GROUP + i
                steps[t] = steps[jnp.clip(link_at[0, t], 0, slots)] + products[i]
            return 0

        return lax.fori_loop(0, PART // GROUP, group, 0)

    lax.fori_loop(0, slots // PART, part, 0)

    ins[6].wait()
    for k in range(half):
        near_copy(k, far_high(k) * 2 + 1 - low).wait_recv()

    def out_copy(i):
        return pltpu.make_async_copy(partial.at[i], partial_hbm.at[i], out_sem.at[i])

    hub_all = hub[...].reshape(blocks * hub_dev, width)
    per = CHUNK // TB

    def finish_rows(i, _):
        summed = jnp.dot(adj[i], hub_all, preferred_element_type=jnp.float32)
        for r in range(per):
            partial[i, r * TB : (r + 1) * TB] = (
                summed[r * TB : (r + 1) * TB] + steps[jnp.clip(last_at[0, i * per + r], 0, slots)]
            )
        out_copy(i).start()
        return 0

    lax.fori_loop(0, row_blocks // per, finish_rows, 0)

    for k in range(1, half):
        far_copy(k, b).wait_send()
    for k in range(half):
        near_copy(k, far_high(k) * 2 + low).wait_send()

    def finish(at, _):
        j = at // blocks
        k = lax.rem(at, blocks)
        src_g = lax.rem(g + groups - j, groups)
        src_b = lax.rem(b + 2 * blocks - half - k, blocks)

        @pl.when((src_g != g) | (src_b != b))
        def _():
            arrived = boundary_copy(
                j, k, lax.rem(g + j, groups), lax.rem(b + half + k, blocks), src_g * blocks + src_b
            )
            arrived.wait_send()
            arrived.wait_recv()

        return 0

    lax.fori_loop(0, devices, finish, 0)
    own.wait()

    def drain(i, _):
        out_copy(i).wait()
        return 0

    lax.fori_loop(0, row_blocks // per, drain, 0)


def layer_kernel(
    count_ref, row_ref, col_ref, received_hbm, partial_hbm, tiles_hbm, weight_hbm,
    out_hbm,
    received, tiles, weight, total, result, picked, in_sem, part_sem, tile_sem, out_sem,
):
    row_blocks = total.shape[0] - 1
    per = CHUNK // TB
    chunks = row_blocks // per
    live = count_ref[0]

    ins = [
        pltpu.make_async_copy(received_hbm, received, in_sem.at[0]),
        pltpu.make_async_copy(weight_hbm, weight, in_sem.at[1]),
    ]

    def part_copy(i):
        at = pl.ds(i * per, per)
        return pltpu.make_async_copy(partial_hbm.at[at], total.at[at], part_sem.at[i])

    for copy in ins:
        copy.start()

    def tile_copy(t, n):
        return pltpu.make_async_copy(tiles_hbm.at[t], tiles.at[n], tile_sem.at[n])

    def collect(t, n):
        remote = col_ref[t] >= row_blocks

        @pl.when(remote)
        def _():
            picked[n] = t
            tile_copy(t, n).start()

        return n + remote.astype(jnp.int32)

    for i in range(chunks):
        part_copy(i).start()
    number = lax.fori_loop(0, live, collect, 0)
    for copy in ins:
        copy.wait()
    for i in range(chunks):
        part_copy(i).wait()

    @pl.loop(0, (number + GROUP - 1) // GROUP)
    def _(u):
        for i in range(GROUP):
            n = u * GROUP + i

            @pl.when(n < number)
            def _():
                tile_copy(picked[n], n).wait()

        products = []
        places = []
        for i in range(GROUP):
            n = u * GROUP + i
            t = picked[jnp.minimum(n, number - 1)]
            block = received[col_ref[t] - row_blocks]
            products.append(jnp.dot(tiles[n], block, preferred_element_type=jnp.float32))
            places.append(jnp.where(n < number, row_ref[t], row_blocks))
        for product, place in zip(products, places):
            total[place] += product

    def out_copy(i):
        at = pl.ds(i * CHUNK, CHUNK)
        return pltpu.make_async_copy(result.at[at], out_hbm.at[at], out_sem.at[i])

    for i in range(chunks):
        rows = total[i * per : (i + 1) * per].reshape(CHUNK, total.shape[2])
        mixed = jnp.dot(rows.astype(jnp.bfloat16), weight[...], preferred_element_type=jnp.float32)
        result[i * CHUNK : (i + 1) * CHUNK, :] = jnp.maximum(mixed, 0.0).astype(jnp.bfloat16)
        out_copy(i).start()
    for i in range(chunks):
        out_copy(i).wait()


def per_device(
    groups, blocks, features, hub_rows, hub_adjacency, tile_row, tile_col, tile_count,
    tile_values, send_rows, weight,
):
    local = features[0, 0]
    rows, width = local.shape
    entries = send_rows.shape[-1]
    hub_dev = hub_rows.shape[-1]
    hubs = blocks * hub_dev
    devices = groups * blocks
    slots = tile_row.shape[-1]
    row_blocks = rows // TB
    chunks = rows // CHUNK
    half = blocks // 2
    bf16 = jnp.bfloat16
    f32 = jnp.float32
    i32 = jnp.int32
    dma = pltpu.SemaphoreType.DMA
    received, partial = pl.pallas_call(
        functools.partial(exchange_kernel, groups, blocks),
        out_shape=(
            jax.ShapeDtypeStruct((devices, entries, width), bf16),
            jax.ShapeDtypeStruct((chunks, CHUNK, width), f32),
        ),
        in_specs=[SMEM] + [ANY] * 7,
        out_specs=(ANY, ANY),
        scratch_shapes=[
            pltpu.VMEM((row_blocks, TB, width), bf16),
            pltpu.VMEM((1, hub_dev), i32),
            pltpu.VMEM((groups, blocks, entries), i32),
            pltpu.VMEM((chunks, CHUNK, hubs), bf16),
            pltpu.VMEM((1, slots), i32),
            pltpu.VMEM((1, slots), i32),
            pltpu.SMEM((1, slots), i32),
            pltpu.VMEM((slots, TB, TB), bf16),
            pltpu.VMEM((1, slots), i32),
            pltpu.VMEM((1, slots), i32),
            pltpu.SMEM((1, slots), i32),
            pltpu.SMEM((1, slots), i32),
            pltpu.VMEM((devices, entries, width), bf16),
            pltpu.VMEM((blocks, hub_dev, width), bf16),
            pltpu.VMEM((slots + 1, TB, width), f32),
            pltpu.VMEM((chunks, CHUNK, width), f32),
            dma((7,)),
            dma((slots // PART,)),
            dma((2,)),
            dma((chunks,)),
            dma(()),
            dma((groups, blocks)),
            dma((groups, blocks)),
            dma((half,)),
            dma((half,)),
            dma((half,)),
            dma((half,)),
        ],
        compiler_params=pltpu.CompilerParams(
            collective_id=0, has_side_effects=True, vmem_limit_bytes=60 << 20
        ),
        name="exchange",
    )(
        tile_count[0], local.reshape(row_blocks, TB, width), hub_rows[0], send_rows[0, 0],
        hub_adjacency[0, 0].reshape(chunks, CHUNK, hubs), tile_row[0], tile_col[0], tile_values[0, 0],
    )
    out = pl.pallas_call(
        layer_kernel,
        out_shape=jax.ShapeDtypeStruct((rows, width), bf16),
        in_specs=[SMEM, SMEM, SMEM, ANY, ANY, ANY, ANY],
        out_specs=ANY,
        scratch_shapes=[
            pltpu.VMEM((devices * entries // TB, TB, width), bf16),
            pltpu.VMEM((slots, TB, TB), bf16),
            pltpu.VMEM(weight.shape, bf16),
            pltpu.VMEM((row_blocks + 1, TB, width), f32),
            pltpu.VMEM((rows, width), bf16),
            pltpu.SMEM((slots,), i32),
            dma((2,)),
            dma((chunks,)),
            dma((slots,)),
            dma((chunks,)),
        ],
        compiler_params=pltpu.CompilerParams(vmem_limit_bytes=60 << 20),
        name="layer",
    )(
        tile_count[0], tile_row[0, 0], tile_col[0, 0],
        received.reshape(devices * entries // TB, TB, width),
        partial.reshape(row_blocks, TB, width), tile_values[0, 0], weight,
    )
    return out[None, None]


def solution(mesh):
    return jax.shard_map(
        functools.partial(per_device, mesh.shape["grp"], mesh.shape["blk"]),
        mesh=mesh,
        in_specs=(
            P("grp", "blk", None, None),
            P("grp", "blk", None),
            P("grp", "blk", None, None),
            P("grp", "blk", None),
            P("grp", "blk", None),
            P("grp", "blk"),
            P("grp", "blk", None, None, None),
            P("grp", "blk", None, None, None),
            P(),
        ),
        out_specs=P("grp", "blk", None, None),
        check_vma=False,
    )
```

```python
import functools

import jax
import jax.numpy as jnp
from jax import lax
from jax.experimental import pallas as pl
from jax.experimental.pallas import tpu as pltpu
from jax.sharding import PartitionSpec as P

TB = 128
MESH = pl.DeviceIdType.MESH
ANY = pl.BlockSpec(memory_space=pl.ANY)
VMEM = pl.BlockSpec(memory_space=pltpu.VMEM)
SMEM = pl.BlockSpec(memory_space=pltpu.SMEM)

PART = 16
GROUP = 4
CHUNK = 512


def pick(listing, feats, arrive=None):
    lists, entries = listing.shape
    blocks, _, width = feats.shape
    count = lists * entries
    wide = jnp.broadcast_to(listing[:, :, None], (lists, entries, CHUNK)).reshape(count, CHUNK)
    offset = wide - lax.broadcasted_iota(jnp.int32, (count, CHUNK), 1)
    total = jnp.zeros((count, width), jnp.float32)
    step = CHUNK // TB
    for at in range(0, blocks, step):
        if arrive is not None:
            arrive(at)
        chosen = jnp.where(offset == at * TB, 1.0, 0.0).astype(jnp.bfloat16)
        part = feats[at : at + step].reshape(CHUNK, width)
        total += jnp.dot(chosen, part, preferred_element_type=jnp.float32)
    return total.astype(jnp.bfloat16)


def exchange_kernel(
    groups, blocks, count_ref, feats_hbm, hub_rows_hbm, send_rows_hbm, adj_hbm, row_hbm, col_hbm, tiles_hbm,
    received_ref, partial_hbm,
    feats, hub_rows, send_rows, adj, row_list, col_list, col_at, tiles,
    links, last, firsts, seconds, link_at, last_at, first_at, second_at,
    stage, hub, steps, partial,
    in_sem, feats_sem, tile_sem, link_sem, out_sem, own_sem,
    send_sem, recv_sem, far_send, far_recv, near_send, near_recv,
):
    g = lax.axis_index("grp")
    b = lax.axis_index("blk")
    entries = send_rows.shape[2]
    hub_dev = hub.shape[1]
    row_blocks, _, width = feats.shape
    slots = row_list.shape[1]
    half = blocks // 2
    me = g * blocks + b
    devices = groups * blocks
    high = b // 2
    low = lax.rem(b, 2)

    barrier = pltpu.get_barrier_semaphore()

    def greet(off, _):
        other = lax.rem(me + off, devices)
        pl.semaphore_signal(
            barrier, inc=1, device_id=(other // blocks, lax.rem(other, blocks)), device_id_type=MESH
        )
        return 0

    ins = [
        pltpu.make_async_copy(hub_rows_hbm, hub_rows, in_sem.at[0]),
        pltpu.make_async_copy(send_rows_hbm, send_rows, in_sem.at[1]),
        pltpu.make_async_copy(row_hbm, row_list, in_sem.at[2]),
        pltpu.make_async_copy(col_hbm, col_list, in_sem.at[3]),
        pltpu.make_async_copy(col_hbm, col_at, in_sem.at[4]),
        pltpu.make_async_copy(adj_hbm, adj, in_sem.at[5]),
    ]

    def tile_copy(c):
        at = pl.ds(c * PART, PART)
        return pltpu.make_async_copy(tiles_hbm.at[at], tiles.at[at], tile_sem.at[c])

    quarter = row_blocks // 4

    def feats_copy(i):
        at = pl.ds(i * quarter, quarter)
        return pltpu.make_async_copy(feats_hbm.at[at], feats.at[at], feats_sem.at[i])

    def arrive(at):
        if at % quarter == 0:
            feats_copy(at // quarter).wait()

    for copy in ins[:2]:
        copy.start()
    for i in range(4):
        feats_copy(i).start()
    for copy in ins[2:5]:
        copy.start()
    lax.fori_loop(1, devices, greet, 0)
    for copy in ins[:2]:
        copy.wait()

    def boundary_copy(j, k, dst_g, dst_b, slot):
        return pltpu.make_async_remote_copy(
            src_ref=stage.at[dst_g * blocks + dst_b],
            dst_ref=received_ref.at[slot],
            send_sem=send_sem.at[j, k],
            recv_sem=recv_sem.at[j, k],
            device_id=(dst_g, dst_b),
            device_id_type=MESH,
        )

    def far_high(k):
        return lax.rem(high + half - k, half)

    def far_copy(k, block):
        return pltpu.make_async_remote_copy(
            src_ref=hub.at[block],
            dst_ref=hub.at[block],
            send_sem=far_send.at[k],
            recv_sem=far_recv.at[k],
            device_id=(g, lax.rem(high + k, half) * 2 + low),
            device_id_type=MESH,
        )

    def near_copy(k, block):
        return pltpu.make_async_remote_copy(
            src_ref=hub.at[block],
            dst_ref=hub.at[block],
            send_sem=near_send.at[k],
            recv_sem=near_recv.at[k],
            device_id=(g, high * 2 + 1 - low),
            device_id_type=MESH,
        )

    def place(dst_g, rows):
        stage[pl.ds(dst_g * blocks, blocks)] = rows.reshape(blocks, entries, width)

    def send(j, dst_g):
        def one(k, _):
            dst_b = lax.rem(b + half + k, blocks)

            @pl.when((dst_g != g) | (dst_b != b))
            def _():
                boundary_copy(j, k, dst_g, dst_b, me).start()

            return 0

        lax.fori_loop(0, blocks, one, 0)

    def chunk(j, _):
        dst_g = lax.rem(g + j, groups)
        place(dst_g, pick(send_rows[dst_g], feats))
        send(j, dst_g)
        return 0

    first_g = lax.rem(g + 1, groups)
    rows = pick(jnp.concatenate([send_rows[first_g], hub_rows[...]], 0), feats, arrive)
    place(first_g, rows[: blocks * entries])
    hub[b] = rows[blocks * entries :]
    pl.semaphore_wait(barrier, devices - 1)
    for k in range(1, half):
        far_copy(k, b).start()
    near_copy(0, b).start()
    send(1, first_g)
    ins[5].start()
    for c in range(slots // PART):
        tile_copy(c).start()
    lax.fori_loop(2, groups, chunk, 0)
    chunk(0, 0)
    own = pltpu.make_async_copy(stage.at[me], received_ref.at[me], own_sem)
    own.start()

    for copy in ins[2:5]:
        copy.wait()
    pairs = link_at.shape[1]
    live = (lax.broadcasted_iota(jnp.int32, (1, slots), 1) < count_ref[0]) & (col_list[...] < row_blocks)
    key = jnp.where(live, row_list[...], row_blocks)
    key_down = jnp.broadcast_to(key[:, :, None], (1, slots, slots)).reshape(slots, slots)
    down = lax.broadcasted_iota(jnp.int32, (slots, slots), 0)
    across = lax.broadcasted_iota(jnp.int32, (slots, slots), 1)

    def tally(hit, axis):
        return jnp.sum(jnp.where(hit, 1, 0), axis=axis, keepdims=True)

    same = key_down == key
    rank_across = tally(same & (down < across), 0)
    rank_down = tally(same & (across < down), 1)
    opens = lax.rem(rank_across, 2) == 0
    before = tally((key < key_down) & opens, 1)
    code = jnp.where(key_down[:, :1] < row_blocks, 2 * before + rank_down, -1)

    def pick_slot(which, value, none):
        found = jnp.max(jnp.where(which, value, -1), axis=0, keepdims=True)
        return jnp.where(found < 0, none, found)

    wanted = 2 * lax.broadcasted_iota(jnp.int32, (slots, pairs), 1)
    slot = lax.broadcasted_iota(jnp.int32, (slots, pairs), 0)
    code = jnp.broadcast_to(code, (slots, pairs))
    firsts[...] = pick_slot(code == wanted, slot, slots)
    seconds[...] = pick_slot(code == wanted + 1, slot, slots)
    rank_wide = jnp.broadcast_to(rank_down, (slots, pairs))
    links[...] = pick_slot((code == wanted) & (rank_wide > 0), wanted // 2 - 1, pairs)
    row_at = lax.broadcasted_iota(jnp.int32, (slots, pairs), 1)
    key_wide = jnp.broadcast_to(key[:, :, None], (1, slots, pairs)).reshape(slots, pairs)
    last[...] = pick_slot(key_wide == row_at, code // 2, pairs)
    to_smem = [
        pltpu.make_async_copy(links, link_at, link_sem.at[0]),
        pltpu.make_async_copy(last, last_at, link_sem.at[1]),
        pltpu.make_async_copy(firsts, first_at, link_sem.at[2]),
        pltpu.make_async_copy(seconds, second_at, link_sem.at[3]),
    ]
    for copy in to_smem:
        copy.start()

    for k in range(1, half):
        block = far_high(k) * 2 + low
        far_copy(k, block).wait_recv()
        near_copy(k, block).start()

    steps[pairs] = jnp.zeros((TB, width), jnp.float32)
    tiles[slots] = jnp.zeros((TB, TB), tiles.dtype)
    for copy in to_smem:
        copy.wait()
    for c in range(slots // PART):
        tile_copy(c).wait()

    def slot_block(t):
        return feats[jnp.clip(col_at[0, jnp.clip(t, 0, slots - 1)], 0, row_blocks - 1)]

    def group(u, _):
        products = []
        for i in range(GROUP):
            n = u * GROUP + i
            one = jnp.clip(first_at[0, n], 0, slots)
            two = jnp.clip(second_at[0, n], 0, slots)
            weights = jnp.concatenate([tiles[one], tiles[two]], 1)
            blocks_in = jnp.concatenate([slot_block(one), slot_block(two)], 0)
            products.append(jnp.dot(weights, blocks_in, preferred_element_type=jnp.float32))
        for i in range(GROUP):
            n = u * GROUP + i
            steps[n] = steps[jnp.clip(link_at[0, n], 0, pairs)] + products[i]
        return 0

    lax.fori_loop(0, pairs // GROUP, group, 0)

    ins[5].wait()
    for k in range(half):
        near_copy(k, far_high(k) * 2 + 1 - low).wait_recv()

    def out_copy(i):
        return pltpu.make_async_copy(partial.at[i], partial_hbm.at[i], out_sem.at[i])

    hub_all = hub[...].reshape(blocks * hub_dev, width)
    per = CHUNK // TB

    def finish_rows(i, _):
        summed = jnp.dot(adj[i], hub_all, preferred_element_type=jnp.float32)
        for r in range(per):
            partial[i, r * TB : (r + 1) * TB] = (
                summed[r * TB : (r + 1) * TB] + steps[jnp.clip(last_at[0, i * per + r], 0, pairs)]
            )
        out_copy(i).start()
        return 0

    lax.fori_loop(0, row_blocks // per, finish_rows, 0)

    for k in range(1, half):
        far_copy(k, b).wait_send()
    for k in range(half):
        near_copy(k, far_high(k) * 2 + low).wait_send()

    def finish(at, _):
        j = at // blocks
        k = lax.rem(at, blocks)
        src_g = lax.rem(g + groups - j, groups)
        src_b = lax.rem(b + 2 * blocks - half - k, blocks)

        @pl.when((src_g != g) | (src_b != b))
        def _():
            arrived = boundary_copy(
                j, k, lax.rem(g + j, groups), lax.rem(b + half + k, blocks), src_g * blocks + src_b
            )
            arrived.wait_send()
            arrived.wait_recv()

        return 0

    lax.fori_loop(0, devices, finish, 0)
    own.wait()

    def drain(i, _):
        out_copy(i).wait()
        return 0

    lax.fori_loop(0, row_blocks // per, drain, 0)


def layer_kernel(
    count_ref, row_ref, col_ref, received_hbm, partial_hbm, tiles_hbm, weight_hbm,
    out_hbm,
    received, tiles, weight, total, result, picked, in_sem, part_sem, tile_sem, out_sem,
):
    row_blocks = total.shape[0] - 1
    per = CHUNK // TB
    chunks = row_blocks // per
    live = count_ref[0]

    ins = [
        pltpu.make_async_copy(received_hbm, received, in_sem.at[0]),
        pltpu.make_async_copy(weight_hbm, weight, in_sem.at[1]),
    ]

    def part_copy(i):
        at = pl.ds(i * per, per)
        return pltpu.make_async_copy(partial_hbm.at[at], total.at[at], part_sem.at[i])

    for copy in ins:
        copy.start()

    def tile_copy(t, n):
        return pltpu.make_async_copy(tiles_hbm.at[t], tiles.at[n], tile_sem.at[n])

    def collect(t, n):
        remote = col_ref[t] >= row_blocks

        @pl.when(remote)
        def _():
            picked[n] = t
            tile_copy(t, n).start()

        return n + remote.astype(jnp.int32)

    for i in range(chunks):
        part_copy(i).start()
    number = lax.fori_loop(0, live, collect, 0)
    for copy in ins:
        copy.wait()
    for i in range(chunks):
        part_copy(i).wait()

    @pl.loop(0, (number + GROUP - 1) // GROUP)
    def _(u):
        for i in range(GROUP):
            n = u * GROUP + i

            @pl.when(n < number)
            def _():
                tile_copy(picked[n], n).wait()

        products = []
        places = []
        for i in range(GROUP):
            n = u * GROUP + i
            t = picked[jnp.minimum(n, number - 1)]
            block = received[col_ref[t] - row_blocks]
            products.append(jnp.dot(tiles[n], block, preferred_element_type=jnp.float32))
            places.append(jnp.where(n < number, row_ref[t], row_blocks))
        for product, place in zip(products, places):
            total[place] += product

    def out_copy(i):
        at = pl.ds(i * CHUNK, CHUNK)
        return pltpu.make_async_copy(result.at[at], out_hbm.at[at], out_sem.at[i])

    for i in range(chunks):
        rows = total[i * per : (i + 1) * per].reshape(CHUNK, total.shape[2])
        mixed = jnp.dot(rows.astype(jnp.bfloat16), weight[...], preferred_element_type=jnp.float32)
        result[i * CHUNK : (i + 1) * CHUNK, :] = jnp.maximum(mixed, 0.0).astype(jnp.bfloat16)
        out_copy(i).start()
    for i in range(chunks):
        out_copy(i).wait()


def per_device(
    groups, blocks, features, hub_rows, hub_adjacency, tile_row, tile_col, tile_count,
    tile_values, send_rows, weight,
):
    local = features[0, 0]
    rows, width = local.shape
    entries = send_rows.shape[-1]
    hub_dev = hub_rows.shape[-1]
    hubs = blocks * hub_dev
    devices = groups * blocks
    slots = tile_row.shape[-1]
    row_blocks = rows // TB
    chunks = rows // CHUNK
    half = blocks // 2
    pairs = -(-(slots + row_blocks) // (2 * GROUP)) * GROUP
    bf16 = jnp.bfloat16
    f32 = jnp.float32
    i32 = jnp.int32
    dma = pltpu.SemaphoreType.DMA
    received, partial = pl.pallas_call(
        functools.partial(exchange_kernel, groups, blocks),
        out_shape=(
            jax.ShapeDtypeStruct((devices, entries, width), bf16),
            jax.ShapeDtypeStruct((chunks, CHUNK, width), f32),
        ),
        in_specs=[SMEM] + [ANY] * 7,
        out_specs=(ANY, ANY),
        scratch_shapes=[
            pltpu.VMEM((row_blocks, TB, width), bf16),
            pltpu.VMEM((1, hub_dev), i32),
            pltpu.VMEM((groups, blocks, entries), i32),
            pltpu.VMEM((chunks, CHUNK, hubs), bf16),
            pltpu.VMEM((1, slots), i32),
            pltpu.VMEM((1, slots), i32),
            pltpu.SMEM((1, slots), i32),
            pltpu.VMEM((slots + 1, TB, TB), bf16),
            pltpu.VMEM((1, pairs), i32),
            pltpu.VMEM((1, pairs), i32),
            pltpu.VMEM((1, pairs), i32),
            pltpu.VMEM((1, pairs), i32),
            pltpu.SMEM((1, pairs), i32),
            pltpu.SMEM((1, pairs), i32),
            pltpu.SMEM((1, pairs), i32),
            pltpu.SMEM((1, pairs), i32),
            pltpu.VMEM((devices, entries, width), bf16),
            pltpu.VMEM((blocks, hub_dev, width), bf16),
            pltpu.VMEM((pairs + 1, TB, width), f32),
            pltpu.VMEM((chunks, CHUNK, width), f32),
            dma((6,)),
            dma((4,)),
            dma((slots // PART,)),
            dma((4,)),
            dma((chunks,)),
            dma(()),
            dma((groups, blocks)),
            dma((groups, blocks)),
            dma((half,)),
            dma((half,)),
            dma((half,)),
            dma((half,)),
        ],
        compiler_params=pltpu.CompilerParams(
            collective_id=0, has_side_effects=True, vmem_limit_bytes=60 << 20
        ),
        name="exchange",
    )(
        tile_count[0], local.reshape(row_blocks, TB, width), hub_rows[0], send_rows[0, 0],
        hub_adjacency[0, 0].reshape(chunks, CHUNK, hubs), tile_row[0], tile_col[0], tile_values[0, 0],
    )
    out = pl.pallas_call(
        layer_kernel,
        out_shape=jax.ShapeDtypeStruct((rows, width), bf16),
        in_specs=[SMEM, SMEM, SMEM, ANY, ANY, ANY, ANY],
        out_specs=ANY,
        scratch_shapes=[
            pltpu.VMEM((devices * entries // TB, TB, width), bf16),
            pltpu.VMEM((slots, TB, TB), bf16),
            pltpu.VMEM(weight.shape, bf16),
            pltpu.VMEM((row_blocks + 1, TB, width), f32),
            pltpu.VMEM((rows, width), bf16),
            pltpu.SMEM((slots,), i32),
            dma((2,)),
            dma((chunks,)),
            dma((slots,)),
            dma((chunks,)),
        ],
        compiler_params=pltpu.CompilerParams(vmem_limit_bytes=60 << 20),
        name="layer",
    )(
        tile_count[0], tile_row[0, 0], tile_col[0, 0],
        received.reshape(devices * entries // TB, TB, width),
        partial.reshape(row_blocks, TB, width), tile_values[0, 0], weight,
    )
    return out[None, None]


def solution(mesh):
    return jax.shard_map(
        functools.partial(per_device, mesh.shape["grp"], mesh.shape["blk"]),
        mesh=mesh,
        in_specs=(
            P("grp", "blk", None, None),
            P("grp", "blk", None),
            P("grp", "blk", None, None),
            P("grp", "blk", None),
            P("grp", "blk", None),
            P("grp", "blk"),
            P("grp", "blk", None, None, None),
            P("grp", "blk", None, None, None),
            P(),
        ),
        out_specs=P("grp", "blk", None, None),
        check_vma=False,
    )
```

```python
import functools

import jax
import jax.numpy as jnp
from jax import lax
from jax.experimental import pallas as pl
from jax.experimental.pallas import tpu as pltpu
from jax.sharding import PartitionSpec as P

TB = 128
MESH = pl.DeviceIdType.MESH
ANY = pl.BlockSpec(memory_space=pl.ANY)
VMEM = pl.BlockSpec(memory_space=pltpu.VMEM)
SMEM = pl.BlockSpec(memory_space=pltpu.SMEM)

PART = 16
GROUP = 4
CHUNK = 512


def pick(listing, feats, arrive=None):
    lists, entries = listing.shape
    blocks, _, width = feats.shape
    count = lists * entries
    wide = jnp.broadcast_to(listing[:, :, None], (lists, entries, CHUNK)).reshape(count, CHUNK)
    offset = wide - lax.broadcasted_iota(jnp.int32, (count, CHUNK), 1)
    total = jnp.zeros((count, width), jnp.float32)
    step = CHUNK // TB
    for at in range(0, blocks, step):
        if arrive is not None:
            arrive(at)
        chosen = jnp.where(offset == at * TB, 1.0, 0.0).astype(jnp.bfloat16)
        part = feats[at : at + step].reshape(CHUNK, width)
        total += jnp.dot(chosen, part, preferred_element_type=jnp.float32)
    return total.astype(jnp.bfloat16)


def exchange_kernel(
    groups, blocks, count_ref, feats_hbm, hub_rows_hbm, send_rows_hbm, adj_hbm, row_hbm, col_hbm, tiles_hbm,
    received_ref, partial_hbm, plan_hbm,
    feats, hub_rows, send_rows, adj, row_list, col_list, col_at, tiles,
    links, last, firsts, seconds, link_at, last_at, first_at, second_at,
    stage, hub, steps, partial, plan,
    in_sem, feats_sem, tile_sem, link_sem, out_sem, own_sem, plan_sem,
    send_sem, recv_sem, far_send, far_recv, near_send, near_recv,
):
    g = lax.axis_index("grp")
    b = lax.axis_index("blk")
    entries = send_rows.shape[2]
    hub_dev = hub.shape[1]
    row_blocks, _, width = feats.shape
    slots = row_list.shape[1]
    half = blocks // 2
    me = g * blocks + b
    devices = groups * blocks
    high = b // 2
    low = lax.rem(b, 2)

    barrier = pltpu.get_barrier_semaphore()

    def greet(off, _):
        other = lax.rem(me + off, devices)
        pl.semaphore_signal(
            barrier, inc=1, device_id=(other // blocks, lax.rem(other, blocks)), device_id_type=MESH
        )
        return 0

    ins = [
        pltpu.make_async_copy(hub_rows_hbm, hub_rows, in_sem.at[0]),
        pltpu.make_async_copy(send_rows_hbm, send_rows, in_sem.at[1]),
        pltpu.make_async_copy(row_hbm, row_list, in_sem.at[2]),
        pltpu.make_async_copy(col_hbm, col_list, in_sem.at[3]),
        pltpu.make_async_copy(col_hbm, col_at, in_sem.at[4]),
        pltpu.make_async_copy(adj_hbm, adj, in_sem.at[5]),
    ]

    def tile_copy(c):
        at = pl.ds(c * PART, PART)
        return pltpu.make_async_copy(tiles_hbm.at[at], tiles.at[at], tile_sem.at[c])

    quarter = row_blocks // 4

    def feats_copy(i):
        at = pl.ds(i * quarter, quarter)
        return pltpu.make_async_copy(feats_hbm.at[at], feats.at[at], feats_sem.at[i])

    def arrive(at):
        if at % quarter == 0:
            feats_copy(at // quarter).wait()

    for copy in ins[:2]:
        copy.start()
    for i in range(4):
        feats_copy(i).start()
    for copy in ins[2:5]:
        copy.start()
    lax.fori_loop(1, devices, greet, 0)
    for copy in ins[:2]:
        copy.wait()

    def boundary_copy(j, k, dst_g, dst_b, slot):
        return pltpu.make_async_remote_copy(
            src_ref=stage.at[dst_g * blocks + dst_b],
            dst_ref=received_ref.at[slot],
            send_sem=send_sem.at[j, k],
            recv_sem=recv_sem.at[j, k],
            device_id=(dst_g, dst_b),
            device_id_type=MESH,
        )

    def far_high(k):
        return lax.rem(high + half - k, half)

    def far_copy(k, block):
        return pltpu.make_async_remote_copy(
            src_ref=hub.at[block],
            dst_ref=hub.at[block],
            send_sem=far_send.at[k],
            recv_sem=far_recv.at[k],
            device_id=(g, lax.rem(high + k, half) * 2 + low),
            device_id_type=MESH,
        )

    def near_copy(k, block):
        return pltpu.make_async_remote_copy(
            src_ref=hub.at[block],
            dst_ref=hub.at[block],
            send_sem=near_send.at[k],
            recv_sem=near_recv.at[k],
            device_id=(g, high * 2 + 1 - low),
            device_id_type=MESH,
        )

    def place(dst_g, rows):
        stage[pl.ds(dst_g * blocks, blocks)] = rows.reshape(blocks, entries, width)

    def send(j, dst_g):
        def one(k, _):
            off = (1 - lax.rem(k + g, 2)) * half + k // 2
            dst_b = lax.rem(b + off, blocks)

            @pl.when((dst_g != g) | (dst_b != b))
            def _():
                boundary_copy(j, off, dst_g, dst_b, me).start()

            return 0

        lax.fori_loop(0, blocks, one, 0)

    def chunk(j, _):
        dst_g = lax.rem(g + j, groups)
        place(dst_g, pick(send_rows[dst_g], feats))
        send(j, dst_g)
        return 0

    first_g = lax.rem(g + 1, groups)
    rows = pick(jnp.concatenate([send_rows[first_g], hub_rows[...]], 0), feats, arrive)
    place(first_g, rows[: blocks * entries])
    hub[b] = rows[blocks * entries :]
    pl.semaphore_wait(barrier, devices - 1)
    for k in range(1, half):
        far_copy(k, b).start()
    near_copy(0, b).start()
    send(1, first_g)
    ins[5].start()
    for c in range(slots // PART):
        tile_copy(c).start()
    lax.fori_loop(2, groups, chunk, 0)
    chunk(0, 0)
    own = pltpu.make_async_copy(stage.at[me], received_ref.at[me], own_sem)
    own.start()

    for copy in ins[2:5]:
        copy.wait()
    pairs = link_at.shape[1]
    live = (lax.broadcasted_iota(jnp.int32, (1, slots), 1) < count_ref[0]) & (col_list[...] < row_blocks)
    key = jnp.where(live, row_list[...], row_blocks)
    key_down = jnp.broadcast_to(key[:, :, None], (1, slots, slots)).reshape(slots, slots)
    down = lax.broadcasted_iota(jnp.int32, (slots, slots), 0)
    across = lax.broadcasted_iota(jnp.int32, (slots, slots), 1)

    def tally(hit, axis):
        return jnp.sum(jnp.where(hit, 1, 0), axis=axis, keepdims=True)

    same = key_down == key
    rank_across = tally(same & (down < across), 0)
    rank_down = tally(same & (across < down), 1)
    opens = lax.rem(rank_across, 2) == 0
    before = tally((key < key_down) & opens, 1)
    code = jnp.where(key_down[:, :1] < row_blocks, 2 * before + rank_down, -1)

    def pick_slot(which, value, none):
        found = jnp.max(jnp.where(which, value, -1), axis=0, keepdims=True)
        return jnp.where(found < 0, none, found)

    wanted = 2 * lax.broadcasted_iota(jnp.int32, (slots, pairs), 1)
    slot = lax.broadcasted_iota(jnp.int32, (slots, pairs), 0)
    code = jnp.broadcast_to(code, (slots, pairs))
    firsts[...] = pick_slot(code == wanted, slot, slots)
    seconds[...] = pick_slot(code == wanted + 1, slot, slots)
    rank_wide = jnp.broadcast_to(rank_down, (slots, pairs))
    links[...] = pick_slot((code == wanted) & (rank_wide > 0), wanted // 2 - 1, pairs)
    row_at = lax.broadcasted_iota(jnp.int32, (slots, pairs), 1)
    key_wide = jnp.broadcast_to(key[:, :, None], (1, slots, pairs)).reshape(slots, pairs)
    last[...] = pick_slot(key_wide == row_at, code // 2, pairs)

    far = (lax.broadcasted_iota(jnp.int32, (1, slots), 1) < count_ref[0]) & (col_list[...] >= row_blocks)
    far_key = jnp.where(far, row_list[...], row_blocks)

    def column(values):
        return jnp.broadcast_to(values[:, :, None], (1, slots, slots)).reshape(slots, slots)

    far_down = column(far_key)
    position = tally((far_key < far_down) | ((far_key == far_down) & (across < down)), 1)
    here = (jnp.broadcast_to(position, (slots, slots)) == across) & (far_down < row_blocks)
    plan[0:1, :] = pick_slot(here, down, 0)
    plan[1:2, :] = pick_slot(here, far_down, row_blocks)
    plan[2:3, :] = pick_slot(here, column(col_list[...]) - row_blocks, 0)
    plan[3:4, :] = tally(far_down < row_blocks, 0)
    plan_copy = pltpu.make_async_copy(plan, plan_hbm, plan_sem)
    plan_copy.start()
    to_smem = [
        pltpu.make_async_copy(links, link_at, link_sem.at[0]),
        pltpu.make_async_copy(last, last_at, link_sem.at[1]),
        pltpu.make_async_copy(firsts, first_at, link_sem.at[2]),
        pltpu.make_async_copy(seconds, second_at, link_sem.at[3]),
    ]
    for copy in to_smem:
        copy.start()

    for k in range(1, half):
        block = far_high(k) * 2 + low
        far_copy(k, block).wait_recv()
        near_copy(k, block).start()

    steps[pairs] = jnp.zeros((TB, width), jnp.float32)
    tiles[slots] = jnp.zeros((TB, TB), tiles.dtype)
    for copy in to_smem:
        copy.wait()
    for c in range(slots // PART):
        tile_copy(c).wait()

    def slot_block(t):
        return feats[jnp.clip(col_at[0, jnp.clip(t, 0, slots - 1)], 0, row_blocks - 1)]

    def group(u, _):
        products = []
        for i in range(GROUP):
            n = u * GROUP + i
            one = jnp.clip(first_at[0, n], 0, slots)
            two = jnp.clip(second_at[0, n], 0, slots)
            weights = jnp.concatenate([tiles[one], tiles[two]], 1)
            blocks_in = jnp.concatenate([slot_block(one), slot_block(two)], 0)
            products.append(jnp.dot(weights, blocks_in, preferred_element_type=jnp.float32))
        for i in range(GROUP):
            n = u * GROUP + i
            steps[n] = steps[jnp.clip(link_at[0, n], 0, pairs)] + products[i]
        return 0

    lax.fori_loop(0, pairs // GROUP, group, 0)

    ins[5].wait()
    for k in range(half):
        near_copy(k, far_high(k) * 2 + 1 - low).wait_recv()

    def out_copy(i):
        return pltpu.make_async_copy(partial.at[i], partial_hbm.at[i], out_sem.at[i])

    hub_all = hub[...].reshape(blocks * hub_dev, width)
    per = CHUNK // TB

    def finish_rows(i, _):
        summed = jnp.dot(adj[i], hub_all, preferred_element_type=jnp.float32)
        for r in range(per):
            partial[i, r * TB : (r + 1) * TB] = (
                summed[r * TB : (r + 1) * TB] + steps[jnp.clip(last_at[0, i * per + r], 0, pairs)]
            )
        out_copy(i).start()
        return 0

    lax.fori_loop(0, row_blocks // per, finish_rows, 0)

    for k in range(1, half):
        far_copy(k, b).wait_send()
    for k in range(half):
        near_copy(k, far_high(k) * 2 + low).wait_send()

    def finish(at, _):
        j = at // blocks
        k = lax.rem(at, blocks)
        src_g = lax.rem(g + groups - j, groups)
        src_b = lax.rem(b + blocks - k, blocks)

        @pl.when((src_g != g) | (src_b != b))
        def _():
            arrived = boundary_copy(
                j, k, lax.rem(g + j, groups), lax.rem(b + k, blocks), src_g * blocks + src_b
            )
            arrived.wait_send()
            arrived.wait_recv()

        return 0

    lax.fori_loop(0, devices, finish, 0)
    own.wait()
    plan_copy.wait()

    def drain(i, _):
        out_copy(i).wait()
        return 0

    lax.fori_loop(0, row_blocks // per, drain, 0)


def layer_kernel(
    plan_ref, received_hbm, partial_hbm, tiles_hbm, weight_hbm,
    out_hbm,
    received, tiles, weight, total, result, in_sem, part_sem, tile_sem, out_sem,
):
    row_blocks = total.shape[0] - 1
    per = CHUNK // TB
    chunks = row_blocks // per
    number = plan_ref[3, 0]

    ins = [
        pltpu.make_async_copy(received_hbm, received, in_sem.at[0]),
        pltpu.make_async_copy(weight_hbm, weight, in_sem.at[1]),
    ]

    def part_copy(i):
        at = pl.ds(i * per, per)
        return pltpu.make_async_copy(partial_hbm.at[at], total.at[at], part_sem.at[i])

    def tile_copy(n):
        return pltpu.make_async_copy(tiles_hbm.at[plan_ref[0, n]], tiles.at[n], tile_sem.at[n])

    for i in range(chunks):
        part_copy(i).start()
    for copy in ins:
        copy.start()

    @pl.loop(0, number)
    def _(n):
        tile_copy(n).start()

    for copy in ins:
        copy.wait()
    for i in range(chunks):
        part_copy(i).wait()

    @pl.loop(0, (number + GROUP - 1) // GROUP)
    def _(u):
        for i in range(GROUP):
            n = u * GROUP + i

            @pl.when(n < number)
            def _():
                tile_copy(n).wait()

        products = []
        places = []
        for i in range(GROUP):
            n = u * GROUP + i
            block = received[plan_ref[2, n]]
            products.append(jnp.dot(tiles[n], block, preferred_element_type=jnp.float32))
            places.append(plan_ref[1, n])
        for product, place in zip(products, places):
            total[place] += product

    def out_copy(i):
        at = pl.ds(i * CHUNK, CHUNK)
        return pltpu.make_async_copy(result.at[at], out_hbm.at[at], out_sem.at[i])

    for i in range(chunks):
        rows = total[i * per : (i + 1) * per].reshape(CHUNK, total.shape[2])
        mixed = jnp.dot(rows.astype(jnp.bfloat16), weight[...], preferred_element_type=jnp.float32)
        result[i * CHUNK : (i + 1) * CHUNK, :] = jnp.maximum(mixed, 0.0).astype(jnp.bfloat16)
        out_copy(i).start()
    for i in range(chunks):
        out_copy(i).wait()


def per_device(
    groups, blocks, features, hub_rows, hub_adjacency, tile_row, tile_col, tile_count,
    tile_values, send_rows, weight,
):
    local = features[0, 0]
    rows, width = local.shape
    entries = send_rows.shape[-1]
    hub_dev = hub_rows.shape[-1]
    hubs = blocks * hub_dev
    devices = groups * blocks
    slots = tile_row.shape[-1]
    row_blocks = rows // TB
    chunks = rows // CHUNK
    half = blocks // 2
    pairs = -(-(slots + row_blocks) // (2 * GROUP)) * GROUP
    bf16 = jnp.bfloat16
    f32 = jnp.float32
    i32 = jnp.int32
    dma = pltpu.SemaphoreType.DMA
    received, partial, plan = pl.pallas_call(
        functools.partial(exchange_kernel, groups, blocks),
        out_shape=(
            jax.ShapeDtypeStruct((devices, entries, width), bf16),
            jax.ShapeDtypeStruct((chunks, CHUNK, width), f32),
            jax.ShapeDtypeStruct((4, slots), i32),
        ),
        in_specs=[SMEM] + [ANY] * 7,
        out_specs=(ANY, ANY, ANY),
        scratch_shapes=[
            pltpu.VMEM((row_blocks, TB, width), bf16),
            pltpu.VMEM((1, hub_dev), i32),
            pltpu.VMEM((groups, blocks, entries), i32),
            pltpu.VMEM((chunks, CHUNK, hubs), bf16),
            pltpu.VMEM((1, slots), i32),
            pltpu.VMEM((1, slots), i32),
            pltpu.SMEM((1, slots), i32),
            pltpu.VMEM((slots + 1, TB, TB), bf16),
            pltpu.VMEM((1, pairs), i32),
            pltpu.VMEM((1, pairs), i32),
            pltpu.VMEM((1, pairs), i32),
            pltpu.VMEM((1, pairs), i32),
            pltpu.SMEM((1, pairs), i32),
            pltpu.SMEM((1, pairs), i32),
            pltpu.SMEM((1, pairs), i32),
            pltpu.SMEM((1, pairs), i32),
            pltpu.VMEM((devices, entries, width), bf16),
            pltpu.VMEM((blocks, hub_dev, width), bf16),
            pltpu.VMEM((pairs + 1, TB, width), f32),
            pltpu.VMEM((chunks, CHUNK, width), f32),
            pltpu.VMEM((4, slots), i32),
            dma((6,)),
            dma((4,)),
            dma((slots // PART,)),
            dma((4,)),
            dma((chunks,)),
            dma(()),
            dma(()),
            dma((groups, blocks)),
            dma((groups, blocks)),
            dma((half,)),
            dma((half,)),
            dma((half,)),
            dma((half,)),
        ],
        compiler_params=pltpu.CompilerParams(
            collective_id=0, has_side_effects=True, vmem_limit_bytes=60 << 20
        ),
        name="exchange",
    )(
        tile_count[0], local.reshape(row_blocks, TB, width), hub_rows[0], send_rows[0, 0],
        hub_adjacency[0, 0].reshape(chunks, CHUNK, hubs), tile_row[0], tile_col[0], tile_values[0, 0],
    )
    out = pl.pallas_call(
        layer_kernel,
        out_shape=jax.ShapeDtypeStruct((rows, width), bf16),
        in_specs=[SMEM, ANY, ANY, ANY, ANY],
        out_specs=ANY,
        scratch_shapes=[
            pltpu.VMEM((devices * entries // TB, TB, width), bf16),
            pltpu.VMEM((slots, TB, TB), bf16),
            pltpu.VMEM(weight.shape, bf16),
            pltpu.VMEM((row_blocks + 1, TB, width), f32),
            pltpu.VMEM((rows, width), bf16),
            dma((2,)),
            dma((chunks,)),
            dma((slots,)),
            dma((chunks,)),
        ],
        compiler_params=pltpu.CompilerParams(vmem_limit_bytes=60 << 20),
        name="layer",
    )(
        plan, received.reshape(devices * entries // TB, TB, width),
        partial.reshape(row_blocks, TB, width), tile_values[0, 0], weight,
    )
    return out[None, None]


def solution(mesh):
    return jax.shard_map(
        functools.partial(per_device, mesh.shape["grp"], mesh.shape["blk"]),
        mesh=mesh,
        in_specs=(
            P("grp", "blk", None, None),
            P("grp", "blk", None),
            P("grp", "blk", None, None),
            P("grp", "blk", None),
            P("grp", "blk", None),
            P("grp", "blk"),
            P("grp", "blk", None, None, None),
            P("grp", "blk", None, None, None),
            P(),
        ),
        out_specs=P("grp", "blk", None, None),
        check_vma=False,
    )
```

```python
import functools

import jax
import jax.numpy as jnp
from jax import lax
from jax.experimental import pallas as pl
from jax.experimental.pallas import tpu as pltpu
from jax.sharding import PartitionSpec as P

TB = 128
MESH = pl.DeviceIdType.MESH
ANY = pl.BlockSpec(memory_space=pl.ANY)
VMEM = pl.BlockSpec(memory_space=pltpu.VMEM)
SMEM = pl.BlockSpec(memory_space=pltpu.SMEM)

PART = 16
GROUP = 4
DEEP = 4
CHUNK = 512


def pick(listing, feats, arrive=None):
    lists, entries = listing.shape
    blocks, _, width = feats.shape
    count = lists * entries
    wide = jnp.broadcast_to(listing[:, :, None], (lists, entries, CHUNK)).reshape(count, CHUNK)
    offset = wide - lax.broadcasted_iota(jnp.int32, (count, CHUNK), 1)
    total = jnp.zeros((count, width), jnp.float32)
    step = CHUNK // TB
    for at in range(0, blocks, step):
        if arrive is not None:
            arrive(at)
        chosen = jnp.where(offset == at * TB, 1.0, 0.0).astype(jnp.bfloat16)
        part = feats[at : at + step].reshape(CHUNK, width)
        total += jnp.dot(chosen, part, preferred_element_type=jnp.float32)
    return total.astype(jnp.bfloat16)


def exchange_kernel(
    groups, blocks, count_ref, feats_hbm, hub_rows_hbm, send_rows_hbm, adj_hbm, row_hbm, col_hbm, tiles_hbm,
    received_ref, partial_hbm, plan_hbm,
    feats, hub_rows, send_rows, adj, row_list, col_list, col_at, tiles,
    links, last, members, link_at, last_at, member_at,
    stage, hub, steps, partial, plan,
    in_sem, feats_sem, tile_sem, link_sem, out_sem, own_sem, plan_sem,
    send_sem, recv_sem, far_send, far_recv, near_send, near_recv,
):
    g = lax.axis_index("grp")
    b = lax.axis_index("blk")
    entries = send_rows.shape[2]
    hub_dev = hub.shape[1]
    row_blocks, _, width = feats.shape
    slots = row_list.shape[1]
    half = blocks // 2
    me = g * blocks + b
    devices = groups * blocks
    high = b // 2
    low = lax.rem(b, 2)

    barrier = pltpu.get_barrier_semaphore()

    def greet(off, _):
        other = lax.rem(me + off, devices)
        pl.semaphore_signal(
            barrier, inc=1, device_id=(other // blocks, lax.rem(other, blocks)), device_id_type=MESH
        )
        return 0

    ins = [
        pltpu.make_async_copy(hub_rows_hbm, hub_rows, in_sem.at[0]),
        pltpu.make_async_copy(send_rows_hbm, send_rows, in_sem.at[1]),
        pltpu.make_async_copy(row_hbm, row_list, in_sem.at[2]),
        pltpu.make_async_copy(col_hbm, col_list, in_sem.at[3]),
        pltpu.make_async_copy(col_hbm, col_at, in_sem.at[4]),
        pltpu.make_async_copy(adj_hbm, adj, in_sem.at[5]),
    ]

    def tile_copy(c):
        at = pl.ds(c * PART, PART)
        return pltpu.make_async_copy(tiles_hbm.at[at], tiles.at[at], tile_sem.at[c])

    quarter = row_blocks // 4

    def feats_copy(i):
        at = pl.ds(i * quarter, quarter)
        return pltpu.make_async_copy(feats_hbm.at[at], feats.at[at], feats_sem.at[i])

    def arrive(at):
        if at % quarter == 0:
            feats_copy(at // quarter).wait()

    for copy in ins[:2]:
        copy.start()
    for i in range(4):
        feats_copy(i).start()
    for copy in ins[2:5]:
        copy.start()
    lax.fori_loop(1, devices, greet, 0)
    for copy in ins[:2]:
        copy.wait()

    def boundary_copy(j, k, dst_g, dst_b, slot):
        return pltpu.make_async_remote_copy(
            src_ref=stage.at[dst_g * blocks + dst_b],
            dst_ref=received_ref.at[slot],
            send_sem=send_sem.at[j, k],
            recv_sem=recv_sem.at[j, k],
            device_id=(dst_g, dst_b),
            device_id_type=MESH,
        )

    def far_high(k):
        return lax.rem(high + half - k, half)

    def far_copy(k, block):
        return pltpu.make_async_remote_copy(
            src_ref=hub.at[block],
            dst_ref=hub.at[block],
            send_sem=far_send.at[k],
            recv_sem=far_recv.at[k],
            device_id=(g, lax.rem(high + k, half) * 2 + low),
            device_id_type=MESH,
        )

    def near_copy(k, block):
        return pltpu.make_async_remote_copy(
            src_ref=hub.at[block],
            dst_ref=hub.at[block],
            send_sem=near_send.at[k],
            recv_sem=near_recv.at[k],
            device_id=(g, high * 2 + 1 - low),
            device_id_type=MESH,
        )

    def place(dst_g, rows):
        stage[pl.ds(dst_g * blocks, blocks)] = rows.reshape(blocks, entries, width)

    def send(j, dst_g):
        def one(k, _):
            off = (1 - lax.rem(k + g, 2)) * half + k // 2
            dst_b = lax.rem(b + off, blocks)

            @pl.when((dst_g != g) | (dst_b != b))
            def _():
                boundary_copy(j, off, dst_g, dst_b, me).start()

            return 0

        lax.fori_loop(0, blocks, one, 0)

    def chunk(j, _):
        dst_g = lax.rem(g + j, groups)
        place(dst_g, pick(send_rows[dst_g], feats))
        send(j, dst_g)
        return 0

    first_g = lax.rem(g + 1, groups)
    rows = pick(jnp.concatenate([send_rows[first_g], hub_rows[...]], 0), feats, arrive)
    place(first_g, rows[: blocks * entries])
    hub[b] = rows[blocks * entries :]
    pl.semaphore_wait(barrier, devices - 1)
    for k in range(1, half):
        far_copy(k, b).start()
    near_copy(0, b).start()
    send(1, first_g)
    ins[5].start()
    for c in range(slots // PART):
        tile_copy(c).start()
    lax.fori_loop(2, groups, chunk, 0)
    chunk(0, 0)
    own = pltpu.make_async_copy(stage.at[me], received_ref.at[me], own_sem)
    own.start()

    for copy in ins[2:5]:
        copy.wait()
    batches = link_at.shape[1]
    live = (lax.broadcasted_iota(jnp.int32, (1, slots), 1) < count_ref[0]) & (col_list[...] < row_blocks)
    key = jnp.where(live, row_list[...], row_blocks)
    key_down = jnp.broadcast_to(key[:, :, None], (1, slots, slots)).reshape(slots, slots)
    down = lax.broadcasted_iota(jnp.int32, (slots, slots), 0)
    across = lax.broadcasted_iota(jnp.int32, (slots, slots), 1)

    def tally(hit, axis):
        return jnp.sum(jnp.where(hit, 1, 0), axis=axis, keepdims=True)

    same = key_down == key
    rank_across = tally(same & (down < across), 0)
    rank_down = tally(same & (across < down), 1)
    opens = lax.rem(rank_across, DEEP) == 0
    before = tally((key < key_down) & opens, 1)
    code = jnp.where(key_down[:, :1] < row_blocks, DEEP * before + rank_down, -1)

    def pick_slot(which, value, none):
        found = jnp.max(jnp.where(which, value, -1), axis=0, keepdims=True)
        return jnp.where(found < 0, none, found)

    wanted = DEEP * lax.broadcasted_iota(jnp.int32, (slots, batches), 1)
    slot = lax.broadcasted_iota(jnp.int32, (slots, batches), 0)
    code = jnp.broadcast_to(code, (slots, batches))
    for i in range(DEEP):
        members[i : i + 1, :] = pick_slot(code == wanted + i, slot, slots)
    rank_wide = jnp.broadcast_to(rank_down, (slots, batches))
    links[...] = pick_slot((code == wanted) & (rank_wide > 0), wanted // DEEP - 1, batches)
    row_at = lax.broadcasted_iota(jnp.int32, (slots, batches), 1)
    key_wide = jnp.broadcast_to(key[:, :, None], (1, slots, batches)).reshape(slots, batches)
    last[...] = pick_slot(key_wide == row_at, code // DEEP, batches)

    far = (lax.broadcasted_iota(jnp.int32, (1, slots), 1) < count_ref[0]) & (col_list[...] >= row_blocks)
    far_key = jnp.where(far, row_list[...], row_blocks)

    def column(values):
        return jnp.broadcast_to(values[:, :, None], (1, slots, slots)).reshape(slots, slots)

    far_down = column(far_key)
    position = tally((far_key < far_down) | ((far_key == far_down) & (across < down)), 1)
    here = (jnp.broadcast_to(position, (slots, slots)) == across) & (far_down < row_blocks)
    plan[0:1, :] = pick_slot(here, down, 0)
    plan[1:2, :] = pick_slot(here, far_down, row_blocks)
    plan[2:3, :] = pick_slot(here, column(col_list[...]) - row_blocks, 0)
    plan[3:4, :] = tally(far_down < row_blocks, 0)
    plan[4:5, :] = tally(far_down < across * (CHUNK // TB), 0)
    plan_copy = pltpu.make_async_copy(plan, plan_hbm, plan_sem)
    plan_copy.start()
    to_smem = [
        pltpu.make_async_copy(links, link_at, link_sem.at[0]),
        pltpu.make_async_copy(last, last_at, link_sem.at[1]),
        pltpu.make_async_copy(members, member_at, link_sem.at[2]),
    ]
    for copy in to_smem:
        copy.start()

    for k in range(1, half):
        block = far_high(k) * 2 + low
        far_copy(k, block).wait_recv()
        near_copy(k, block).start()

    steps[batches] = jnp.zeros((TB, width), jnp.float32)
    tiles[slots] = jnp.zeros((TB, TB), tiles.dtype)
    for copy in to_smem:
        copy.wait()
    for c in range(slots // PART):
        tile_copy(c).wait()

    def slot_block(t):
        return feats[jnp.clip(col_at[0, jnp.clip(t, 0, slots - 1)], 0, row_blocks - 1)]

    def group(u, _):
        products = []
        for i in range(GROUP):
            n = u * GROUP + i
            those = [jnp.clip(member_at[d, n], 0, slots) for d in range(DEEP)]
            weights = jnp.concatenate([tiles[t] for t in those], 1)
            blocks_in = jnp.concatenate([slot_block(t) for t in those], 0)
            products.append(jnp.dot(weights, blocks_in, preferred_element_type=jnp.float32))
        for i in range(GROUP):
            n = u * GROUP + i
            steps[n] = steps[jnp.clip(link_at[0, n], 0, batches)] + products[i]
        return 0

    lax.fori_loop(0, batches // GROUP, group, 0)

    ins[5].wait()
    for k in range(half):
        near_copy(k, far_high(k) * 2 + 1 - low).wait_recv()

    def out_copy(i):
        return pltpu.make_async_copy(partial.at[i], partial_hbm.at[i], out_sem.at[i])

    hub_all = hub[...].reshape(blocks * hub_dev, width)
    per = CHUNK // TB

    def finish_rows(i, _):
        summed = jnp.dot(adj[i], hub_all, preferred_element_type=jnp.float32)
        for r in range(per):
            partial[i, r * TB : (r + 1) * TB] = (
                summed[r * TB : (r + 1) * TB] + steps[jnp.clip(last_at[0, i * per + r], 0, batches)]
            )
        out_copy(i).start()
        return 0

    lax.fori_loop(0, row_blocks // per, finish_rows, 0)

    for k in range(1, half):
        far_copy(k, b).wait_send()
    for k in range(half):
        near_copy(k, far_high(k) * 2 + low).wait_send()

    def finish(at, _):
        j = at // blocks
        k = lax.rem(at, blocks)
        src_g = lax.rem(g + groups - j, groups)
        src_b = lax.rem(b + blocks - k, blocks)

        @pl.when((src_g != g) | (src_b != b))
        def _():
            arrived = boundary_copy(
                j, k, lax.rem(g + j, groups), lax.rem(b + k, blocks), src_g * blocks + src_b
            )
            arrived.wait_send()
            arrived.wait_recv()

        return 0

    lax.fori_loop(0, devices, finish, 0)
    own.wait()
    plan_copy.wait()

    def drain(i, _):
        out_copy(i).wait()
        return 0

    lax.fori_loop(0, row_blocks // per, drain, 0)


def layer_kernel(
    plan_ref, received_hbm, partial_hbm, tiles_hbm, weight_hbm,
    out_hbm,
    received, tiles, weight, total, result, extra, in_sem, part_sem, tile_sem, out_sem,
):
    row_blocks = total.shape[0]
    per = CHUNK // TB
    chunks = row_blocks // per
    number = plan_ref[3, 0]

    ins = [
        pltpu.make_async_copy(received_hbm, received, in_sem.at[0]),
        pltpu.make_async_copy(weight_hbm, weight, in_sem.at[1]),
    ]

    def part_copy(i):
        at = pl.ds(i * per, per)
        return pltpu.make_async_copy(partial_hbm.at[at], total.at[at], part_sem.at[i])

    def tile_copy(n):
        return pltpu.make_async_copy(tiles_hbm.at[plan_ref[0, n]], tiles.at[n], tile_sem.at[n])

    for copy in ins:
        copy.start()
    part_copy(0).start()

    @pl.loop(0, number)
    def _(n):
        tile_copy(n).start()

    for i in range(1, chunks):
        part_copy(i).start()
    for copy in ins:
        copy.wait()

    @pl.loop(0, (number + GROUP - 1) // GROUP)
    def _(u):
        for i in range(GROUP):
            n = u * GROUP + i

            @pl.when(n < number)
            def _():
                tile_copy(n).wait()

        for i in range(GROUP):
            n = u * GROUP + i
            extra[n] = jnp.dot(
                tiles[n], received[plan_ref[2, n]], preferred_element_type=jnp.float32
            )

    def out_copy(i):
        at = pl.ds(i * CHUNK, CHUNK)
        return pltpu.make_async_copy(result.at[at], out_hbm.at[at], out_sem.at[i])

    for i in range(chunks):
        part_copy(i).wait()

        @pl.loop(plan_ref[4, i], plan_ref[4, i + 1])
        def _(n):
            total[plan_ref[1, n]] += extra[n]

        rows = total[i * per : (i + 1) * per].reshape(CHUNK, total.shape[2])
        mixed = jnp.dot(rows.astype(jnp.bfloat16), weight[...], preferred_element_type=jnp.float32)
        result[i * CHUNK : (i + 1) * CHUNK, :] = jnp.maximum(mixed, 0.0).astype(jnp.bfloat16)
        out_copy(i).start()
    for i in range(chunks):
        out_copy(i).wait()


def per_device(
    groups, blocks, features, hub_rows, hub_adjacency, tile_row, tile_col, tile_count,
    tile_values, send_rows, weight,
):
    local = features[0, 0]
    rows, width = local.shape
    entries = send_rows.shape[-1]
    hub_dev = hub_rows.shape[-1]
    hubs = blocks * hub_dev
    devices = groups * blocks
    slots = tile_row.shape[-1]
    row_blocks = rows // TB
    chunks = rows // CHUNK
    half = blocks // 2
    batches = -(-(slots + (DEEP - 1) * row_blocks) // (DEEP * GROUP)) * GROUP
    bf16 = jnp.bfloat16
    f32 = jnp.float32
    i32 = jnp.int32
    dma = pltpu.SemaphoreType.DMA
    received, partial, plan = pl.pallas_call(
        functools.partial(exchange_kernel, groups, blocks),
        out_shape=(
            jax.ShapeDtypeStruct((devices, entries, width), bf16),
            jax.ShapeDtypeStruct((chunks, CHUNK, width), f32),
            jax.ShapeDtypeStruct((5, slots), i32),
        ),
        in_specs=[SMEM] + [ANY] * 7,
        out_specs=(ANY, ANY, ANY),
        scratch_shapes=[
            pltpu.VMEM((row_blocks, TB, width), bf16),
            pltpu.VMEM((1, hub_dev), i32),
            pltpu.VMEM((groups, blocks, entries), i32),
            pltpu.VMEM((chunks, CHUNK, hubs), bf16),
            pltpu.VMEM((1, slots), i32),
            pltpu.VMEM((1, slots), i32),
            pltpu.SMEM((1, slots), i32),
            pltpu.VMEM((slots + 1, TB, TB), bf16),
            pltpu.VMEM((1, batches), i32),
            pltpu.VMEM((1, batches), i32),
            pltpu.VMEM((DEEP, batches), i32),
            pltpu.SMEM((1, batches), i32),
            pltpu.SMEM((1, batches), i32),
            pltpu.SMEM((DEEP, batches), i32),
            pltpu.VMEM((devices, entries, width), bf16),
            pltpu.VMEM((blocks, hub_dev, width), bf16),
            pltpu.VMEM((batches + 1, TB, width), f32),
            pltpu.VMEM((chunks, CHUNK, width), f32),
            pltpu.VMEM((5, slots), i32),
            dma((6,)),
            dma((4,)),
            dma((slots // PART,)),
            dma((3,)),
            dma((chunks,)),
            dma(()),
            dma(()),
            dma((groups, blocks)),
            dma((groups, blocks)),
            dma((half,)),
            dma((half,)),
            dma((half,)),
            dma((half,)),
        ],
        compiler_params=pltpu.CompilerParams(
            collective_id=0, has_side_effects=True, vmem_limit_bytes=60 << 20
        ),
        name="exchange",
    )(
        tile_count[0], local.reshape(row_blocks, TB, width), hub_rows[0], send_rows[0, 0],
        hub_adjacency[0, 0].reshape(chunks, CHUNK, hubs), tile_row[0], tile_col[0], tile_values[0, 0],
    )
    out = pl.pallas_call(
        layer_kernel,
        out_shape=jax.ShapeDtypeStruct((rows, width), bf16),
        in_specs=[SMEM, ANY, ANY, ANY, ANY],
        out_specs=ANY,
        scratch_shapes=[
            pltpu.VMEM((devices * entries // TB, TB, width), bf16),
            pltpu.VMEM((slots, TB, TB), bf16),
            pltpu.VMEM(weight.shape, bf16),
            pltpu.VMEM((row_blocks, TB, width), f32),
            pltpu.VMEM((rows, width), bf16),
            pltpu.VMEM((slots, TB, width), f32),
            dma((2,)),
            dma((chunks,)),
            dma((slots,)),
            dma((chunks,)),
        ],
        compiler_params=pltpu.CompilerParams(vmem_limit_bytes=60 << 20),
        name="layer",
    )(
        plan, received.reshape(devices * entries // TB, TB, width),
        partial.reshape(row_blocks, TB, width), tile_values[0, 0], weight,
    )
    return out[None, None]


def solution(mesh):
    return jax.shard_map(
        functools.partial(per_device, mesh.shape["grp"], mesh.shape["blk"]),
        mesh=mesh,
        in_specs=(
            P("grp", "blk", None, None),
            P("grp", "blk", None),
            P("grp", "blk", None, None),
            P("grp", "blk", None),
            P("grp", "blk", None),
            P("grp", "blk"),
            P("grp", "blk", None, None, None),
            P("grp", "blk", None, None, None),
            P(),
        ),
        out_specs=P("grp", "blk", None, None),
        check_vma=False,
    )
```

```python
import functools

import jax
import jax.numpy as jnp
from jax import lax
from jax.experimental import pallas as pl
from jax.experimental.pallas import tpu as pltpu
from jax.sharding import PartitionSpec as P

TB = 128
MESH = pl.DeviceIdType.MESH
ANY = pl.BlockSpec(memory_space=pl.ANY)
SMEM = pl.BlockSpec(memory_space=pltpu.SMEM)

PART = 16
GROUP = 4
CHUNK = 512


def pick(listing, feats, arrive=None):
    lists, entries = listing.shape
    blocks, _, width = feats.shape
    count = lists * entries
    wide = jnp.broadcast_to(listing[:, :, None], (lists, entries, CHUNK)).reshape(count, CHUNK)
    offset = wide - lax.broadcasted_iota(jnp.int32, (count, CHUNK), 1)
    total = jnp.zeros((count, width), jnp.float32)
    step = CHUNK // TB
    for at in range(0, blocks, step):
        if arrive is not None:
            arrive(at)
        chosen = jnp.where(offset == at * TB, 1.0, 0.0).astype(jnp.bfloat16)
        part = feats[at : at + step].reshape(CHUNK, width)
        total += jnp.dot(chosen, part, preferred_element_type=jnp.float32)
    return total.astype(jnp.bfloat16)


def exchange_kernel(
    groups, blocks, count_ref, feats_hbm, hub_rows_hbm, send_rows_hbm, adj_hbm, row_hbm, col_hbm, tiles_hbm,
    received_ref, partial_hbm, plan_hbm,
    feats, hub_rows, send_rows, adj, row_list, col_list, col_at, tiles,
    links, last, firsts, seconds, link_at, last_at, first_at, second_at,
    stage, hub, steps, partial, plan,
    in_sem, feats_sem, tile_sem, link_sem, out_sem, own_sem, plan_sem,
    send_sem, recv_sem, far_send, far_recv, near_send, near_recv,
):
    g = lax.axis_index("grp")
    b = lax.axis_index("blk")
    entries = send_rows.shape[2]
    hub_dev = hub.shape[1]
    row_blocks, _, width = feats.shape
    slots = row_list.shape[1]
    half = blocks // 2
    me = g * blocks + b
    devices = groups * blocks
    high = b // 2
    low = lax.rem(b, 2)

    barrier = pltpu.get_barrier_semaphore()

    def greet(off, _):
        other = lax.rem(me + off, devices)
        pl.semaphore_signal(
            barrier, inc=1, device_id=(other // blocks, lax.rem(other, blocks)), device_id_type=MESH
        )
        return 0

    ins = [
        pltpu.make_async_copy(hub_rows_hbm, hub_rows, in_sem.at[0]),
        pltpu.make_async_copy(send_rows_hbm, send_rows, in_sem.at[1]),
        pltpu.make_async_copy(row_hbm, row_list, in_sem.at[2]),
        pltpu.make_async_copy(col_hbm, col_list, in_sem.at[3]),
        pltpu.make_async_copy(col_hbm, col_at, in_sem.at[4]),
        pltpu.make_async_copy(adj_hbm, adj, in_sem.at[5]),
    ]

    def tile_copy(c):
        at = pl.ds(c * PART, PART)
        return pltpu.make_async_copy(tiles_hbm.at[at], tiles.at[at], tile_sem.at[c])

    quarter = row_blocks // 4

    def feats_copy(i):
        at = pl.ds(i * quarter, quarter)
        return pltpu.make_async_copy(feats_hbm.at[at], feats.at[at], feats_sem.at[i])

    def arrive(at):
        if at % quarter == 0:
            feats_copy(at // quarter).wait()

    for copy in ins[:2]:
        copy.start()
    for i in range(4):
        feats_copy(i).start()
    for copy in ins[2:5]:
        copy.start()
    lax.fori_loop(1, devices, greet, 0)
    for copy in ins[:2]:
        copy.wait()

    def boundary_copy(j, k, dst_g, dst_b, slot):
        return pltpu.make_async_remote_copy(
            src_ref=stage.at[dst_g * blocks + dst_b],
            dst_ref=received_ref.at[slot],
            send_sem=send_sem.at[j, k],
            recv_sem=recv_sem.at[j, k],
            device_id=(dst_g, dst_b),
            device_id_type=MESH,
        )

    def far_high(k):
        return lax.rem(high + half - k, half)

    def far_copy(k, block):
        return pltpu.make_async_remote_copy(
            src_ref=hub.at[block],
            dst_ref=hub.at[block],
            send_sem=far_send.at[k],
            recv_sem=far_recv.at[k],
            device_id=(g, lax.rem(high + k, half) * 2 + low),
            device_id_type=MESH,
        )

    def near_copy(k, block):
        return pltpu.make_async_remote_copy(
            src_ref=hub.at[block],
            dst_ref=hub.at[block],
            send_sem=near_send.at[k],
            recv_sem=near_recv.at[k],
            device_id=(g, high * 2 + 1 - low),
            device_id_type=MESH,
        )

    def place(dst_g, rows):
        stage[pl.ds(dst_g * blocks, blocks)] = rows.reshape(blocks, entries, width)

    def send(j, dst_g):
        def one(k, _):
            off = (1 - lax.rem(k + g, 2)) * half + k // 2
            dst_b = lax.rem(b + off, blocks)

            @pl.when((dst_g != g) | (dst_b != b))
            def _():
                boundary_copy(j, off, dst_g, dst_b, me).start()

            return 0

        lax.fori_loop(0, blocks, one, 0)

    def chunk(j, _):
        dst_g = lax.rem(g + j, groups)
        place(dst_g, pick(send_rows[dst_g], feats))
        send(j, dst_g)
        return 0

    first_g = lax.rem(g + 1, groups)
    rows = pick(jnp.concatenate([send_rows[first_g], hub_rows[...]], 0), feats, arrive)
    place(first_g, rows[: blocks * entries])
    hub[b] = rows[blocks * entries :]
    pl.semaphore_wait(barrier, devices - 1)
    for k in range(1, half):
        far_copy(k, b).start()
    near_copy(0, b).start()
    send(1, first_g)
    ins[5].start()
    for c in range(slots // PART):
        tile_copy(c).start()
    lax.fori_loop(2, groups, chunk, 0)
    chunk(0, 0)
    own = pltpu.make_async_copy(stage.at[me], received_ref.at[me], own_sem)
    own.start()

    for copy in ins[2:5]:
        copy.wait()
    pairs = link_at.shape[1]
    live = (lax.broadcasted_iota(jnp.int32, (1, slots), 1) < count_ref[0]) & (col_list[...] < row_blocks)
    key = jnp.where(live, row_list[...], row_blocks)
    key_down = jnp.broadcast_to(key[:, :, None], (1, slots, slots)).reshape(slots, slots)
    down = lax.broadcasted_iota(jnp.int32, (slots, slots), 0)
    across = lax.broadcasted_iota(jnp.int32, (slots, slots), 1)

    def tally(hit, axis):
        return jnp.sum(jnp.where(hit, 1, 0), axis=axis, keepdims=True)

    same = key_down == key
    rank_across = tally(same & (down < across), 0)
    rank_down = tally(same & (across < down), 1)
    opens = lax.rem(rank_across, 2) == 0
    before = tally((key < key_down) & opens, 1)
    code = jnp.where(key_down[:, :1] < row_blocks, 2 * before + rank_down, -1)

    def pick_slot(which, value, none):
        found = jnp.max(jnp.where(which, value, -1), axis=0, keepdims=True)
        return jnp.where(found < 0, none, found)

    wanted = 2 * lax.broadcasted_iota(jnp.int32, (slots, pairs), 1)
    slot = lax.broadcasted_iota(jnp.int32, (slots, pairs), 0)
    code = jnp.broadcast_to(code, (slots, pairs))
    firsts[...] = pick_slot(code == wanted, slot, slots)
    seconds[...] = pick_slot(code == wanted + 1, slot, slots)
    rank_wide = jnp.broadcast_to(rank_down, (slots, pairs))
    links[...] = pick_slot((code == wanted) & (rank_wide > 0), wanted // 2 - 1, pairs)
    row_at = lax.broadcasted_iota(jnp.int32, (slots, pairs), 1)
    key_wide = jnp.broadcast_to(key[:, :, None], (1, slots, pairs)).reshape(slots, pairs)
    last[...] = pick_slot(key_wide == row_at, code // 2, pairs)

    far = (lax.broadcasted_iota(jnp.int32, (1, slots), 1) < count_ref[0]) & (col_list[...] >= row_blocks)
    far_key = jnp.where(far, row_list[...], row_blocks)

    def column(values):
        return jnp.broadcast_to(values[:, :, None], (1, slots, slots)).reshape(slots, slots)

    far_down = column(far_key)
    position = tally((far_key < far_down) | ((far_key == far_down) & (across < down)), 1)
    here = (jnp.broadcast_to(position, (slots, slots)) == across) & (far_down < row_blocks)
    plan[0:1, :] = pick_slot(here, down, 0)
    plan[1:2, :] = pick_slot(here, far_down, row_blocks)
    plan[2:3, :] = pick_slot(here, column(col_list[...]) - row_blocks, 0)
    plan[3:4, :] = tally(far_down < row_blocks, 0)
    plan_copy = pltpu.make_async_copy(plan, plan_hbm, plan_sem)
    plan_copy.start()
    to_smem = [
        pltpu.make_async_copy(links, link_at, link_sem.at[0]),
        pltpu.make_async_copy(last, last_at, link_sem.at[1]),
        pltpu.make_async_copy(firsts, first_at, link_sem.at[2]),
        pltpu.make_async_copy(seconds, second_at, link_sem.at[3]),
    ]
    for copy in to_smem:
        copy.start()

    for k in range(1, half):
        block = far_high(k) * 2 + low
        far_copy(k, block).wait_recv()
        near_copy(k, block).start()

    steps[pairs] = jnp.zeros((TB, width), jnp.float32)
    tiles[slots] = jnp.zeros((TB, TB), tiles.dtype)
    for copy in to_smem:
        copy.wait()
    for c in range(slots // PART):
        tile_copy(c).wait()

    def slot_block(t):
        return feats[jnp.clip(col_at[0, jnp.clip(t, 0, slots - 1)], 0, row_blocks - 1)]

    def group(u, _):
        products = []
        for i in range(GROUP):
            n = u * GROUP + i
            one = jnp.clip(first_at[0, n], 0, slots)
            two = jnp.clip(second_at[0, n], 0, slots)
            weights = jnp.concatenate([tiles[one], tiles[two]], 1)
            blocks_in = jnp.concatenate([slot_block(one), slot_block(two)], 0)
            products.append(jnp.dot(weights, blocks_in, preferred_element_type=jnp.float32))
        for i in range(GROUP):
            n = u * GROUP + i
            steps[n] = steps[jnp.clip(link_at[0, n], 0, pairs)] + products[i]
        return 0

    lax.fori_loop(0, pairs // GROUP, group, 0)

    ins[5].wait()
    for k in range(half):
        near_copy(k, far_high(k) * 2 + 1 - low).wait_recv()

    def out_copy(i):
        return pltpu.make_async_copy(partial.at[i], partial_hbm.at[i], out_sem.at[i])

    hub_all = hub[...].reshape(blocks * hub_dev, width)
    per = CHUNK // TB

    def finish_rows(i, _):
        summed = jnp.dot(adj[i], hub_all, preferred_element_type=jnp.float32)
        for r in range(per):
            partial[i, r * TB : (r + 1) * TB] = (
                summed[r * TB : (r + 1) * TB] + steps[jnp.clip(last_at[0, i * per + r], 0, pairs)]
            )
        out_copy(i).start()
        return 0

    lax.fori_loop(0, row_blocks // per, finish_rows, 0)

    for k in range(1, half):
        far_copy(k, b).wait_send()
    for k in range(half):
        near_copy(k, far_high(k) * 2 + low).wait_send()

    def finish(at, _):
        j = at // blocks
        k = lax.rem(at, blocks)
        src_g = lax.rem(g + groups - j, groups)
        src_b = lax.rem(b + blocks - k, blocks)

        @pl.when((src_g != g) | (src_b != b))
        def _():
            arrived = boundary_copy(
                j, k, lax.rem(g + j, groups), lax.rem(b + k, blocks), src_g * blocks + src_b
            )
            arrived.wait_send()
            arrived.wait_recv()

        return 0

    lax.fori_loop(0, devices, finish, 0)
    own.wait()
    plan_copy.wait()

    def drain(i, _):
        out_copy(i).wait()
        return 0

    lax.fori_loop(0, row_blocks // per, drain, 0)


def layer_kernel(
    plan_hbm, received_hbm, partial_hbm, tiles_hbm, weight_hbm,
    out_hbm,
    received, tiles, weight, total, result, plan_ref, in_sem, part_sem, tile_sem, out_sem,
):
    row_blocks = total.shape[0] - 1
    per = CHUNK // TB
    chunks = row_blocks // per

    ins = [
        pltpu.make_async_copy(received_hbm, received, in_sem.at[0]),
        pltpu.make_async_copy(weight_hbm, weight, in_sem.at[1]),
    ]

    def part_copy(i):
        at = pl.ds(i * per, per)
        return pltpu.make_async_copy(partial_hbm.at[at], total.at[at], part_sem.at[i])

    def tile_copy(n):
        return pltpu.make_async_copy(tiles_hbm.at[plan_ref[0, n]], tiles.at[n], tile_sem.at[n])

    plan_copy = pltpu.make_async_copy(plan_hbm, plan_ref, in_sem.at[2])
    plan_copy.start()
    for copy in ins:
        copy.start()
    for i in range(chunks):
        part_copy(i).start()
    plan_copy.wait()
    number = plan_ref[3, 0]

    @pl.loop(0, number)
    def _(n):
        tile_copy(n).start()

    for copy in ins:
        copy.wait()
    for i in range(chunks):
        part_copy(i).wait()

    @pl.loop(0, (number + GROUP - 1) // GROUP)
    def _(u):
        for i in range(GROUP):
            n = u * GROUP + i

            @pl.when(n < number)
            def _():
                tile_copy(n).wait()

        products = []
        places = []
        for i in range(GROUP):
            n = u * GROUP + i
            block = received[plan_ref[2, n]]
            products.append(jnp.dot(tiles[n], block, preferred_element_type=jnp.float32))
            places.append(plan_ref[1, n])
        for product, place in zip(products, places):
            total[place] += product

    def out_copy(i):
        at = pl.ds(i * CHUNK, CHUNK)
        return pltpu.make_async_copy(result.at[at], out_hbm.at[at], out_sem.at[i])

    for i in range(chunks):
        rows = total[i * per : (i + 1) * per].reshape(CHUNK, total.shape[2])
        mixed = jnp.dot(rows.astype(jnp.bfloat16), weight[...], preferred_element_type=jnp.float32)
        result[i * CHUNK : (i + 1) * CHUNK, :] = jnp.maximum(mixed, 0.0).astype(jnp.bfloat16)
        out_copy(i).start()
    for i in range(chunks):
        out_copy(i).wait()


def per_device(
    groups, blocks, features, hub_rows, hub_adjacency, tile_row, tile_col, tile_count,
    tile_values, send_rows, weight,
):
    local = features[0, 0]
    rows, width = local.shape
    entries = send_rows.shape[-1]
    hub_dev = hub_rows.shape[-1]
    hubs = blocks * hub_dev
    devices = groups * blocks
    slots = tile_row.shape[-1]
    row_blocks = rows // TB
    chunks = rows // CHUNK
    half = blocks // 2
    pairs = -(-(slots + row_blocks) // (2 * GROUP)) * GROUP
    bf16 = jnp.bfloat16
    f32 = jnp.float32
    i32 = jnp.int32
    dma = pltpu.SemaphoreType.DMA
    received, partial, plan = pl.pallas_call(
        functools.partial(exchange_kernel, groups, blocks),
        out_shape=(
            jax.ShapeDtypeStruct((devices, entries, width), bf16),
            jax.ShapeDtypeStruct((chunks, CHUNK, width), f32),
            jax.ShapeDtypeStruct((4, slots), i32),
        ),
        in_specs=[SMEM] + [ANY] * 7,
        out_specs=(ANY, ANY, ANY),
        scratch_shapes=[
            pltpu.VMEM((row_blocks, TB, width), bf16),
            pltpu.VMEM((1, hub_dev), i32),
            pltpu.VMEM((groups, blocks, entries), i32),
            pltpu.VMEM((chunks, CHUNK, hubs), bf16),
            pltpu.VMEM((1, slots), i32),
            pltpu.VMEM((1, slots), i32),
            pltpu.SMEM((1, slots), i32),
            pltpu.VMEM((slots + 1, TB, TB), bf16),
            pltpu.VMEM((1, pairs), i32),
            pltpu.VMEM((1, pairs), i32),
            pltpu.VMEM((1, pairs), i32),
            pltpu.VMEM((1, pairs), i32),
            pltpu.SMEM((1, pairs), i32),
            pltpu.SMEM((1, pairs), i32),
            pltpu.SMEM((1, pairs), i32),
            pltpu.SMEM((1, pairs), i32),
            pltpu.VMEM((devices, entries, width), bf16),
            pltpu.VMEM((blocks, hub_dev, width), bf16),
            pltpu.VMEM((pairs + 1, TB, width), f32),
            pltpu.VMEM((chunks, CHUNK, width), f32),
            pltpu.VMEM((4, slots), i32),
            dma((6,)),
            dma((4,)),
            dma((slots // PART,)),
            dma((4,)),
            dma((chunks,)),
            dma(()),
            dma(()),
            dma((groups, blocks)),
            dma((groups, blocks)),
            dma((half,)),
            dma((half,)),
            dma((half,)),
            dma((half,)),
        ],
        compiler_params=pltpu.CompilerParams(
            collective_id=0, has_side_effects=True, vmem_limit_bytes=60 << 20
        ),
        name="exchange",
    )(
        tile_count[0], local.reshape(row_blocks, TB, width), hub_rows[0], send_rows[0, 0],
        hub_adjacency[0, 0].reshape(chunks, CHUNK, hubs), tile_row[0], tile_col[0], tile_values[0, 0],
    )
    out = pl.pallas_call(
        layer_kernel,
        out_shape=jax.ShapeDtypeStruct((rows, width), bf16),
        in_specs=[ANY] * 5,
        out_specs=ANY,
        scratch_shapes=[
            pltpu.VMEM((devices * entries // TB, TB, width), bf16),
            pltpu.VMEM((slots, TB, TB), bf16),
            pltpu.VMEM(weight.shape, bf16),
            pltpu.VMEM((row_blocks + 1, TB, width), f32),
            pltpu.VMEM((rows, width), bf16),
            pltpu.SMEM((4, slots), i32),
            dma((3,)),
            dma((chunks,)),
            dma((slots,)),
            dma((chunks,)),
        ],
        compiler_params=pltpu.CompilerParams(vmem_limit_bytes=60 << 20),
        name="layer",
    )(
        plan, received.reshape(devices * entries // TB, TB, width),
        partial.reshape(row_blocks, TB, width), tile_values[0, 0], weight,
    )
    return out[None, None]


def solution(mesh):
    return jax.shard_map(
        functools.partial(per_device, mesh.shape["grp"], mesh.shape["blk"]),
        mesh=mesh,
        in_specs=(
            P("grp", "blk", None, None),
            P("grp", "blk", None),
            P("grp", "blk", None, None),
            P("grp", "blk", None),
            P("grp", "blk", None),
            P("grp", "blk"),
            P("grp", "blk", None, None, None),
            P("grp", "blk", None, None, None),
            P(),
        ),
        out_specs=P("grp", "blk", None, None),
        check_vma=False,
    )
```

```python
import functools

import jax
import jax.numpy as jnp
from jax import lax
from jax.experimental import pallas as pl
from jax.experimental.pallas import tpu as pltpu
from jax.sharding import PartitionSpec as P

TB = 128
MESH = pl.DeviceIdType.MESH
ANY = pl.BlockSpec(memory_space=pl.ANY)
SMEM = pl.BlockSpec(memory_space=pltpu.SMEM)

PART = 16
GROUP = 4
FAR_GROUP = 8
CHUNK = 512


def pick(listing, feats, arrive=None):
    lists, entries = listing.shape
    blocks, _, width = feats.shape
    count = lists * entries
    wide = jnp.broadcast_to(listing[:, :, None], (lists, entries, CHUNK)).reshape(count, CHUNK)
    offset = wide - lax.broadcasted_iota(jnp.int32, (count, CHUNK), 1)
    total = jnp.zeros((count, width), jnp.float32)
    step = CHUNK // TB
    for at in range(0, blocks, step):
        if arrive is not None:
            arrive(at)
        chosen = jnp.where(offset == at * TB, 1.0, 0.0).astype(jnp.bfloat16)
        part = feats[at : at + step].reshape(CHUNK, width)
        total += jnp.dot(chosen, part, preferred_element_type=jnp.float32)
    return total.astype(jnp.bfloat16)


def exchange_kernel(
    groups, blocks, count_ref, feats_hbm, hub_rows_hbm, send_rows_hbm, adj_hbm, row_hbm, col_hbm, tiles_hbm,
    received_ref, partial_hbm, plan_hbm,
    feats, hub_rows, send_rows, adj, row_list, col_list, col_at, tiles,
    links, last, firsts, seconds, link_at, last_at, first_at, second_at,
    stage, hub, steps, partial, plan,
    in_sem, feats_sem, tile_sem, link_sem, out_sem, own_sem, plan_sem,
    send_sem, recv_sem, far_send, far_recv, near_send, near_recv,
):
    g = lax.axis_index("grp")
    b = lax.axis_index("blk")
    entries = send_rows.shape[2]
    hub_dev = hub.shape[1]
    row_blocks, _, width = feats.shape
    slots = row_list.shape[1]
    half = blocks // 2
    me = g * blocks + b
    devices = groups * blocks
    high = b // 2
    low = lax.rem(b, 2)

    barrier = pltpu.get_barrier_semaphore()

    def greet(off, _):
        other = lax.rem(me + off, devices)
        pl.semaphore_signal(
            barrier, inc=1, device_id=(other // blocks, lax.rem(other, blocks)), device_id_type=MESH
        )
        return 0

    ins = [
        pltpu.make_async_copy(hub_rows_hbm, hub_rows, in_sem.at[0]),
        pltpu.make_async_copy(send_rows_hbm, send_rows, in_sem.at[1]),
        pltpu.make_async_copy(row_hbm, row_list, in_sem.at[2]),
        pltpu.make_async_copy(col_hbm, col_list, in_sem.at[3]),
        pltpu.make_async_copy(col_hbm, col_at, in_sem.at[4]),
        pltpu.make_async_copy(adj_hbm, adj, in_sem.at[5]),
    ]

    def tile_copy(c):
        at = pl.ds(c * PART, PART)
        return pltpu.make_async_copy(tiles_hbm.at[at], tiles.at[at], tile_sem.at[c])

    quarter = row_blocks // 4

    def feats_copy(i):
        at = pl.ds(i * quarter, quarter)
        return pltpu.make_async_copy(feats_hbm.at[at], feats.at[at], feats_sem.at[i])

    def arrive(at):
        if at % quarter == 0:
            feats_copy(at // quarter).wait()

    for copy in ins[:2]:
        copy.start()
    for i in range(4):
        feats_copy(i).start()
    for copy in ins[2:5]:
        copy.start()
    lax.fori_loop(1, devices, greet, 0)
    for copy in ins[:2]:
        copy.wait()

    def boundary_copy(j, k, dst_g, dst_b, slot):
        return pltpu.make_async_remote_copy(
            src_ref=stage.at[dst_g * blocks + dst_b],
            dst_ref=received_ref.at[slot],
            send_sem=send_sem.at[j, k],
            recv_sem=recv_sem.at[j, k],
            device_id=(dst_g, dst_b),
            device_id_type=MESH,
        )

    def far_high(k):
        return lax.rem(high + half - k, half)

    def far_copy(k, block):
        return pltpu.make_async_remote_copy(
            src_ref=hub.at[block],
            dst_ref=hub.at[block],
            send_sem=far_send.at[k],
            recv_sem=far_recv.at[k],
            device_id=(g, lax.rem(high + k, half) * 2 + low),
            device_id_type=MESH,
        )

    def near_copy(k, block):
        return pltpu.make_async_remote_copy(
            src_ref=hub.at[block],
            dst_ref=hub.at[block],
            send_sem=near_send.at[k],
            recv_sem=near_recv.at[k],
            device_id=(g, high * 2 + 1 - low),
            device_id_type=MESH,
        )

    def place(dst_g, rows):
        stage[pl.ds(dst_g * blocks, blocks)] = rows.reshape(blocks, entries, width)

    def send(j, dst_g):
        def one(k, _):
            off = (1 - lax.rem(k + g, 2)) * half + k // 2
            dst_b = lax.rem(b + off, blocks)

            @pl.when((dst_g != g) | (dst_b != b))
            def _():
                boundary_copy(j, off, dst_g, dst_b, me).start()

            return 0

        lax.fori_loop(0, blocks, one, 0)

    def chunk(j, _):
        dst_g = lax.rem(g + j, groups)
        place(dst_g, pick(send_rows[dst_g], feats))
        send(j, dst_g)
        return 0

    first_g = lax.rem(g + 1, groups)
    rows = pick(jnp.concatenate([send_rows[first_g], hub_rows[...]], 0), feats, arrive)
    place(first_g, rows[: blocks * entries])
    hub[b] = rows[blocks * entries :]
    pl.semaphore_wait(barrier, devices - 1)
    for k in range(1, half):
        far_copy(k, b).start()
    near_copy(0, b).start()
    send(1, first_g)
    ins[5].start()
    for c in range(slots // PART):
        tile_copy(c).start()
    lax.fori_loop(2, groups, chunk, 0)
    chunk(0, 0)
    own = pltpu.make_async_copy(stage.at[me], received_ref.at[me], own_sem)
    own.start()

    for copy in ins[2:5]:
        copy.wait()
    pairs = link_at.shape[1]
    live = (lax.broadcasted_iota(jnp.int32, (1, slots), 1) < count_ref[0]) & (col_list[...] < row_blocks)
    key = jnp.where(live, row_list[...], row_blocks)
    key_down = jnp.broadcast_to(key[:, :, None], (1, slots, slots)).reshape(slots, slots)
    down = lax.broadcasted_iota(jnp.int32, (slots, slots), 0)
    across = lax.broadcasted_iota(jnp.int32, (slots, slots), 1)

    def tally(hit, axis):
        return jnp.sum(jnp.where(hit, 1, 0), axis=axis, keepdims=True)

    same = key_down == key
    rank_across = tally(same & (down < across), 0)
    rank_down = tally(same & (across < down), 1)
    opens = lax.rem(rank_across, 2) == 0
    before = tally((key < key_down) & opens, 1)
    code = jnp.where(key_down[:, :1] < row_blocks, 2 * before + rank_down, -1)

    def pick_slot(which, value, none):
        found = jnp.max(jnp.where(which, value, -1), axis=0, keepdims=True)
        return jnp.where(found < 0, none, found)

    wanted = 2 * lax.broadcasted_iota(jnp.int32, (slots, pairs), 1)
    slot = lax.broadcasted_iota(jnp.int32, (slots, pairs), 0)
    code = jnp.broadcast_to(code, (slots, pairs))
    firsts[...] = pick_slot(code == wanted, slot, slots)
    seconds[...] = pick_slot(code == wanted + 1, slot, slots)
    rank_wide = jnp.broadcast_to(rank_down, (slots, pairs))
    links[...] = pick_slot((code == wanted) & (rank_wide > 0), wanted // 2 - 1, pairs)
    row_at = lax.broadcasted_iota(jnp.int32, (slots, pairs), 1)
    key_wide = jnp.broadcast_to(key[:, :, None], (1, slots, pairs)).reshape(slots, pairs)
    last[...] = pick_slot(key_wide == row_at, code // 2, pairs)

    far = (lax.broadcasted_iota(jnp.int32, (1, slots), 1) < count_ref[0]) & (col_list[...] >= row_blocks)
    far_key = jnp.where(far, row_list[...], row_blocks)

    def column(values):
        return jnp.broadcast_to(values[:, :, None], (1, slots, slots)).reshape(slots, slots)

    far_down = column(far_key)
    position = tally((far_key < far_down) | ((far_key == far_down) & (across < down)), 1)
    here = (jnp.broadcast_to(position, (slots, slots)) == across) & (far_down < row_blocks)
    plan[0:1, :] = pick_slot(here, down, 0)
    plan[1:2, :] = pick_slot(here, far_down, row_blocks)
    plan[2:3, :] = pick_slot(here, column(col_list[...]) - row_blocks, 0)
    plan[3:4, :] = tally(far_down < row_blocks, 0)
    plan_copy = pltpu.make_async_copy(plan, plan_hbm, plan_sem)
    plan_copy.start()
    to_smem = [
        pltpu.make_async_copy(links, link_at, link_sem.at[0]),
        pltpu.make_async_copy(last, last_at, link_sem.at[1]),
        pltpu.make_async_copy(firsts, first_at, link_sem.at[2]),
        pltpu.make_async_copy(seconds, second_at, link_sem.at[3]),
    ]
    for copy in to_smem:
        copy.start()

    for k in range(1, half):
        block = far_high(k) * 2 + low
        far_copy(k, block).wait_recv()
        near_copy(k, block).start()

    steps[pairs] = jnp.zeros((TB, width), jnp.float32)
    tiles[slots] = jnp.zeros((TB, TB), tiles.dtype)
    for copy in to_smem:
        copy.wait()
    for c in range(slots // PART):
        tile_copy(c).wait()

    def slot_block(t):
        return feats[jnp.clip(col_at[0, jnp.clip(t, 0, slots - 1)], 0, row_blocks - 1)]

    def group(u, _):
        products = []
        for i in range(GROUP):
            n = u * GROUP + i
            one = jnp.clip(first_at[0, n], 0, slots)
            two = jnp.clip(second_at[0, n], 0, slots)
            weights = jnp.concatenate([tiles[one], tiles[two]], 1)
            blocks_in = jnp.concatenate([slot_block(one), slot_block(two)], 0)
            products.append(jnp.dot(weights, blocks_in, preferred_element_type=jnp.float32))
        for i in range(GROUP):
            n = u * GROUP + i
            steps[n] = steps[jnp.clip(link_at[0, n], 0, pairs)] + products[i]
        return 0

    lax.fori_loop(0, pairs // GROUP, group, 0)

    ins[5].wait()
    for k in range(half):
        near_copy(k, far_high(k) * 2 + 1 - low).wait_recv()

    def out_copy(i):
        return pltpu.make_async_copy(partial.at[i], partial_hbm.at[i], out_sem.at[i])

    hub_all = hub[...].reshape(blocks * hub_dev, width)
    per = CHUNK // TB

    def finish_rows(i, _):
        summed = jnp.dot(adj[i], hub_all, preferred_element_type=jnp.float32)
        for r in range(per):
            partial[i, r * TB : (r + 1) * TB] = (
                summed[r * TB : (r + 1) * TB] + steps[jnp.clip(last_at[0, i * per + r], 0, pairs)]
            )
        out_copy(i).start()
        return 0

    lax.fori_loop(0, row_blocks // per, finish_rows, 0)

    for k in range(1, half):
        far_copy(k, b).wait_send()
    for k in range(half):
        near_copy(k, far_high(k) * 2 + low).wait_send()

    def finish(at, _):
        j = at // blocks
        k = lax.rem(at, blocks)
        src_g = lax.rem(g + groups - j, groups)
        src_b = lax.rem(b + blocks - k, blocks)

        @pl.when((src_g != g) | (src_b != b))
        def _():
            arrived = boundary_copy(
                j, k, lax.rem(g + j, groups), lax.rem(b + k, blocks), src_g * blocks + src_b
            )
            arrived.wait_send()
            arrived.wait_recv()

        return 0

    lax.fori_loop(0, devices, finish, 0)
    own.wait()
    plan_copy.wait()

    def drain(i, _):
        out_copy(i).wait()
        return 0

    lax.fori_loop(0, row_blocks // per, drain, 0)


def layer_kernel(
    plan_hbm, received_hbm, partial_hbm, tiles_hbm, weight_hbm,
    out_hbm,
    received, tiles, weight, total, result, plan_ref, in_sem, part_sem, tile_sem, out_sem,
):
    row_blocks = total.shape[0] - 1
    per = CHUNK // TB
    chunks = row_blocks // per

    ins = [
        pltpu.make_async_copy(received_hbm, received, in_sem.at[0]),
        pltpu.make_async_copy(weight_hbm, weight, in_sem.at[1]),
    ]

    def part_copy(i):
        at = pl.ds(i * per, per)
        return pltpu.make_async_copy(partial_hbm.at[at], total.at[at], part_sem.at[i])

    def tile_copy(n):
        return pltpu.make_async_copy(tiles_hbm.at[plan_ref[0, n]], tiles.at[n], tile_sem.at[n])

    plan_copy = pltpu.make_async_copy(plan_hbm, plan_ref, in_sem.at[2])
    plan_copy.start()
    for copy in ins:
        copy.start()
    for i in range(chunks):
        part_copy(i).start()
    plan_copy.wait()
    number = plan_ref[3, 0]

    @pl.loop(0, number)
    def _(n):
        tile_copy(n).start()

    for copy in ins:
        copy.wait()
    for i in range(chunks):
        part_copy(i).wait()

    @pl.loop(0, (number + FAR_GROUP - 1) // FAR_GROUP)
    def _(u):
        for i in range(FAR_GROUP):
            n = u * FAR_GROUP + i

            @pl.when(n < number)
            def _():
                tile_copy(n).wait()

        products = []
        places = []
        for i in range(FAR_GROUP):
            n = u * FAR_GROUP + i
            block = received[plan_ref[2, n]]
            products.append(jnp.dot(tiles[n], block, preferred_element_type=jnp.float32))
            places.append(plan_ref[1, n])
        for product, place in zip(products, places):
            total[place] += product

    def out_copy(i):
        at = pl.ds(i * CHUNK, CHUNK)
        return pltpu.make_async_copy(result.at[at], out_hbm.at[at], out_sem.at[i])

    for i in range(chunks):
        rows = total[i * per : (i + 1) * per].reshape(CHUNK, total.shape[2])
        mixed = jnp.dot(rows.astype(jnp.bfloat16), weight[...], preferred_element_type=jnp.float32)
        result[i * CHUNK : (i + 1) * CHUNK, :] = jnp.maximum(mixed, 0.0).astype(jnp.bfloat16)
        out_copy(i).start()
    for i in range(chunks):
        out_copy(i).wait()


def per_device(
    groups, blocks, features, hub_rows, hub_adjacency, tile_row, tile_col, tile_count,
    tile_values, send_rows, weight,
):
    local = features[0, 0]
    rows, width = local.shape
    entries = send_rows.shape[-1]
    hub_dev = hub_rows.shape[-1]
    hubs = blocks * hub_dev
    devices = groups * blocks
    slots = tile_row.shape[-1]
    row_blocks = rows // TB
    chunks = rows // CHUNK
    half = blocks // 2
    pairs = -(-(slots + row_blocks) // (2 * GROUP)) * GROUP
    bf16 = jnp.bfloat16
    f32 = jnp.float32
    i32 = jnp.int32
    dma = pltpu.SemaphoreType.DMA
    received, partial, plan = pl.pallas_call(
        functools.partial(exchange_kernel, groups, blocks),
        out_shape=(
            jax.ShapeDtypeStruct((devices, entries, width), bf16),
            jax.ShapeDtypeStruct((chunks, CHUNK, width), f32),
            jax.ShapeDtypeStruct((4, slots), i32),
        ),
        in_specs=[SMEM] + [ANY] * 7,
        out_specs=(ANY, ANY, ANY),
        scratch_shapes=[
            pltpu.VMEM((row_blocks, TB, width), bf16),
            pltpu.VMEM((1, hub_dev), i32),
            pltpu.VMEM((groups, blocks, entries), i32),
            pltpu.VMEM((chunks, CHUNK, hubs), bf16),
            pltpu.VMEM((1, slots), i32),
            pltpu.VMEM((1, slots), i32),
            pltpu.SMEM((1, slots), i32),
            pltpu.VMEM((slots + 1, TB, TB), bf16),
            pltpu.VMEM((1, pairs), i32),
            pltpu.VMEM((1, pairs), i32),
            pltpu.VMEM((1, pairs), i32),
            pltpu.VMEM((1, pairs), i32),
            pltpu.SMEM((1, pairs), i32),
            pltpu.SMEM((1, pairs), i32),
            pltpu.SMEM((1, pairs), i32),
            pltpu.SMEM((1, pairs), i32),
            pltpu.VMEM((devices, entries, width), bf16),
            pltpu.VMEM((blocks, hub_dev, width), bf16),
            pltpu.VMEM((pairs + 1, TB, width), f32),
            pltpu.VMEM((chunks, CHUNK, width), f32),
            pltpu.VMEM((4, slots), i32),
            dma((6,)),
            dma((4,)),
            dma((slots // PART,)),
            dma((4,)),
            dma((chunks,)),
            dma(()),
            dma(()),
            dma((groups, blocks)),
            dma((groups, blocks)),
            dma((half,)),
            dma((half,)),
            dma((half,)),
            dma((half,)),
        ],
        compiler_params=pltpu.CompilerParams(
            collective_id=0, has_side_effects=True, vmem_limit_bytes=60 << 20
        ),
        name="exchange",
    )(
        tile_count[0], local.reshape(row_blocks, TB, width), hub_rows[0], send_rows[0, 0],
        hub_adjacency[0, 0].reshape(chunks, CHUNK, hubs), tile_row[0], tile_col[0], tile_values[0, 0],
    )
    out = pl.pallas_call(
        layer_kernel,
        out_shape=jax.ShapeDtypeStruct((rows, width), bf16),
        in_specs=[ANY] * 5,
        out_specs=ANY,
        scratch_shapes=[
            pltpu.VMEM((devices * entries // TB, TB, width), bf16),
            pltpu.VMEM((slots, TB, TB), bf16),
            pltpu.VMEM(weight.shape, bf16),
            pltpu.VMEM((row_blocks + 1, TB, width), f32),
            pltpu.VMEM((rows, width), bf16),
            pltpu.SMEM((4, slots), i32),
            dma((3,)),
            dma((chunks,)),
            dma((slots,)),
            dma((chunks,)),
        ],
        compiler_params=pltpu.CompilerParams(vmem_limit_bytes=60 << 20),
        name="layer",
    )(
        plan, received.reshape(devices * entries // TB, TB, width),
        partial.reshape(row_blocks, TB, width), tile_values[0, 0], weight,
    )
    return out[None, None]


def solution(mesh):
    return jax.shard_map(
        functools.partial(per_device, mesh.shape["grp"], mesh.shape["blk"]),
        mesh=mesh,
        in_specs=(
            P("grp", "blk", None, None),
            P("grp", "blk", None),
            P("grp", "blk", None, None),
            P("grp", "blk", None),
            P("grp", "blk", None),
            P("grp", "blk"),
            P("grp", "blk", None, None, None),
            P("grp", "blk", None, None, None),
            P(),
        ),
        out_specs=P("grp", "blk", None, None),
        check_vma=False,
    )
```
